32 devices in a mesh: grp: 4 (over y, x), seq: 8 (over z, core).
Axes of the slice: x: 2, y: 2, z: 4, core: 2. Of those that a mesh axis runs over, the one named last changes fastest.
Arguments:
- grad_output: bfloat16 [1024, 8192], P('seq', 'grp'), may hold values from -6 to 6
- hidden: bfloat16 [1024, 28672], P('seq', 'grp'), may hold values from -6 to 6
- down_weight: bfloat16 [28672, 8192], P('seq', 'grp'), may hold values from -0.0625 to 0.0625
- adapter_down: bfloat16 [16, 64, 28672], P(None, None, ('grp', 'seq')), may hold values from -0.03125 to 0.03125
- adapter_up: bfloat16 [16, 64, 8192], P(None, None, ('grp', 'seq')), may hold values from -0.0625 to 0.0625
- job_tenant: int32 [8, 4], replicated, may hold values from 0 to 15, all different within a row
- job_count: int32 [8, 4], replicated, may hold values from 1 to 64, 128 in all within a row
Outputs:
- grad_hidden: bfloat16 [1024, 28672], P('seq', 'grp')
- grad_adapter_down: float32 [16, 64, 28672], P(None, None, ('grp', 'seq'))
- grad_adapter_up: float32 [16, 64, 8192], P(None, None, ('grp', 'seq'))
The draws below stay inside these ranges and needn't reach their ends.
Inputs may be any that keep to these rules, and one draw needn't show every extreme that they name: `job_tenant`: each row names 4 different tenants; every tenant is named by some row. `job_count`: each row sums to 128, and its largest entry is exactly 64.
All inputs are finite; a program needn't handle non-finite values.
Results may differ from the reference program's by a relative error of at most 0.015.
Values may be sent and summed in bfloat16 or wider, within the bound.
No kernel may reach another device: no remote copies, remote signals or barrier semaphores. Data moves between devices by JAX's collectives and lax.ppermute only.
A program may use at most 128 MiB of HBM per device.

```python
import math
import jax
import jax.numpy as jnp
import numpy as np
from jax import lax

D = 8192
FF = 28672
R = 64
TOK_DEV = 128
JOBS = 4
JOB_MOST = 64
TOKENS = 1024
TENANTS = 16
N_GRP = 4
N_SEQ = 8


def block_scale(stream_key, dims, shards, least, top_value):
    factor_of, own = 1.0, jax.random.fold_in(stream_key, 6)
    for axis_at, parts in shards:
        draws = jnp.exp(jax.random.uniform(jax.random.fold_in(own, axis_at), (parts,), jnp.float32, least / len(shards), top_value / len(shards)))
        factor_of = factor_of * jnp.repeat(draws, dims[axis_at] // parts).reshape([-1 if axis == axis_at else 1 for axis in range(len(dims))])
    return factor_of


def picks_of(key, rows, number_of, top, lift):
    ranking = jax.random.permutation(jax.random.fold_in(key, 1), number_of)
    favour = ranking
    for power in range(3):
        favour = favour * favour // number_of
    favour = favour * lift // number_of
    chance = jax.random.randint(jax.random.fold_in(key, 2), (rows, number_of), 0, 4096) + favour
    holders = jax.random.permutation(jax.random.fold_in(key, 3), rows)[jnp.arange(number_of) % rows]
    chance = jnp.where(jnp.arange(rows)[:, None] == holders[None, :], 1 << 14, chance)
    score = chance * number_of + jnp.arange(number_of)
    return lax.top_k(score.astype(jnp.int32), top)[1].astype(jnp.int32)


def split_up(number_of, total, reach, slope):
    portions = [(1 << 20) // math.isqrt(rank ** slope) + 1 for rank in range(2, number_of + 1)]
    surplus, given = total - reach - (number_of - 1), [1] * (number_of - 1)
    while surplus > 0:
        movable = [i for i in range(number_of - 1) if given[i] < reach]
        pool, budget = sum([portions[i] for i in movable]), surplus
        for i in movable:
            addition = min(reach - given[i], max(1, budget * portions[i] // pool), surplus)
            given[i] = given[i] + addition
            surplus = surplus - addition
    return np.array([reach] + given)


def ragged_sizes(stream_key, number_of, total, limit, lean):
    if number_of == 2:
        one = jax.random.randint(stream_key, (), max(1, total - limit), min(limit, total - 1) + 1)
        return jnp.stack([one, total - one])
    tallies = jnp.asarray(split_up(number_of, total, limit, lean), jnp.int32)
    pairs = (number_of - 1) // 2
    donor, taker = tallies[1:1 + 2 * pairs:2], tallies[2:2 + 2 * pairs:2]
    margin = jnp.minimum(donor - 1, limit - taker)
    shifted = jax.random.randint(jax.random.fold_in(stream_key, 1), (pairs,), 0, 1 << 20) % (margin + 1)
    tallies = tallies.at[1:1 + 2 * pairs:2].set(donor - shifted).at[2:2 + 2 * pairs:2].set(taker + shifted)
    return tallies[jax.random.permutation(jax.random.fold_in(stream_key, 2), number_of)]


def scatter_about(stream_key, dims, width, limit, shards=(), held_as=jnp.bfloat16):
    loudness = block_scale(stream_key, dims, shards, -0.22, 0.18) if shards else 1.0
    result = jax.random.normal(stream_key, dims, jnp.float32) * width * loudness
    return jnp.minimum(jnp.maximum(result, -limit), limit).astype(held_as)


def setup_inputs(seed: int = 0) -> dict:
    splits = jax.random.split(jax.random.key(seed), 8)
    grad_output = scatter_about(splits[0], (TOKENS, D), 1.0, 6.0, ((0, 8), (1, 4)))
    hidden = scatter_about(splits[1], (TOKENS, FF), 1.0, 6.0, ((0, 8), (1, 4)))
    down_weight = scatter_about(splits[2], (FF, D), D ** -0.5, 0.0625, ((0, 8), (1, 4)))
    adapter_down = scatter_about(splits[3], (TENANTS, R, FF), FF ** -0.5, 0.03125, ((2, 32),))
    adapter_up = scatter_about(splits[4], (TENANTS, R, D), D ** -0.5, 0.0625, ((2, 32),))
    job_tenant = picks_of(splits[5], N_SEQ, TENANTS, JOBS, 4096)
    job_count = jax.vmap(lambda own: ragged_sizes(own, JOBS, TOK_DEV, JOB_MOST, 1))(jax.random.split(splits[6], N_SEQ)).reshape((N_SEQ, JOBS)).astype(jnp.int32)
    return {"grad_output": grad_output, "hidden": hidden, "down_weight": down_weight, "adapter_down": adapter_down, "adapter_up": adapter_up, "job_tenant": job_tenant, "job_count": job_count}


ADAPTER_SCALE = 2.0


def settle(value):
    return lax.optimization_barrier(value.astype(jnp.bfloat16)).astype(jnp.float32)


def reference(grad_output, hidden, down_weight, adapter_down, adapter_up, job_tenant, job_count):
    width_d = D // N_GRP
    width_f = FF // N_GRP
    base_sum = jnp.zeros((TOKENS, FF), jnp.float32)
    for group in range(N_GRP):
        columns = slice(group * width_d, (group + 1) * width_d)
        partial_value = lax.dot_general(grad_output[:, columns], down_weight[:, columns],
                                  (((1,), (1,)), ((), ())), preferred_element_type=jnp.float32)
        base_sum = base_sum + settle(partial_value)
    base_grad = base_sum.astype(jnp.bfloat16)

    tenant_table = (job_tenant[:, :, None] == jnp.arange(TENANTS, dtype=jnp.int32)[None, None, :]).astype(jnp.float32)
    totals = jnp.sum(job_count.astype(jnp.float32)[:, :, None] * tenant_table, axis=(0, 1))
    weights = ADAPTER_SCALE / totals
    positions = jnp.arange(TOK_DEV, dtype=jnp.int32)

    def shard(carry, inputs):
        grad_down, grad_up = carry
        rows_out, rows_hidden, rows_base, tenants, counts = inputs
        run_ends = jnp.cumsum(counts)
        run_starts = run_ends - counts
        member = ((positions[:, None] >= run_starts[None, :]) & (positions[:, None] < run_ends[None, :])).astype(jnp.float32)
        down_sel = adapter_down[tenants].astype(jnp.float32)
        up_sel = adapter_up[tenants].astype(jnp.float32)
        out_rows = rows_out.astype(jnp.float32)
        hid_rows = rows_hidden.astype(jnp.float32)
        grad_rank = jnp.zeros((TOK_DEV, R), jnp.float32)
        act_rank = jnp.zeros((TOK_DEV, R), jnp.float32)
        for group in range(N_GRP):
            dcolumns = slice(group * width_d, (group + 1) * width_d)
            fcolumns = slice(group * width_f, (group + 1) * width_f)
            grad_proj = jnp.einsum("td,jrd->tjr", out_rows[:, dcolumns], up_sel[:, :, dcolumns])
            act_proj = jnp.einsum("tf,jrf->tjr", hid_rows[:, fcolumns], down_sel[:, :, fcolumns])
            grad_rank = grad_rank + settle(jnp.sum(grad_proj * member[:, :, None], axis=1))
            act_rank = act_rank + settle(jnp.sum(act_proj * member[:, :, None], axis=1))
        grad_spread = member[:, :, None] * settle(grad_rank)[:, None, :]
        act_spread = member[:, :, None] * settle(act_rank)[:, None, :]
        adapter_term = ADAPTER_SCALE * jnp.einsum("tjr,jrf->tf", grad_spread, down_sel)
        rows_grad = (rows_base.astype(jnp.float32) + adapter_term).astype(jnp.bfloat16)
        job_weights = weights[tenants]
        part_down = settle(job_weights[:, None, None] * jnp.einsum("tjr,tf->jrf", grad_spread, hid_rows))
        part_up = settle(job_weights[:, None, None] * jnp.einsum("tjr,td->jrd", act_spread, out_rows))
        grad_down = grad_down.at[tenants].add(part_down)
        grad_up = grad_up.at[tenants].add(part_up)
        return (grad_down, grad_up), rows_grad

    start = (jnp.zeros((TENANTS, R, FF), jnp.float32), jnp.zeros((TENANTS, R, D), jnp.float32))
    inputs = (grad_output.reshape(N_SEQ, TOK_DEV, D), hidden.reshape(N_SEQ, TOK_DEV, FF),
              base_grad.reshape(N_SEQ, TOK_DEV, FF), job_tenant, job_count)
    (grad_down, grad_up), rows = lax.scan(shard, start, inputs)
    return rows.reshape(TOKENS, FF), grad_down, grad_up
```

```python
import jax
import jax.numpy as jnp
from jax import lax
from jax.sharding import PartitionSpec as P

ADAPTER_SCALE = 2.0
CONTRACT_LAST = (((1,), (1,)), ((), ()))
CONTRACT_ROWS = (((0,), (0,)), ((), ()))
CORES = 2
MOST_ROWS = 1024


def dot(left, right, dims):
    return lax.dot_general(left, right, dims, preferred_element_type=jnp.float32)


def pieces(total):
    step = min(total, MOST_ROWS)
    return [(at, min(step, total - at)) for at in range(0, total, step)]


def project(rows, adapter, mask):
    tenants, ranks, width = adapter.shape
    flat = adapter.reshape(tenants * ranks, width)
    parts = []
    for at, size in pieces(rows.shape[0]):
        full = dot(rows[at : at + size], flat, CONTRACT_LAST)
        chosen = full.reshape(size, tenants, ranks) * mask[at : at + size, :, None]
        parts.append(jnp.sum(chosen, axis=1))
    return jnp.concatenate(parts, axis=0).astype(jnp.bfloat16)


def spread(rank, mask):
    wide = rank[:, None, :] * mask.astype(jnp.bfloat16)[:, :, None]
    return wide.reshape(rank.shape[0], -1)


def adapter_grad(rank, mask, rows, weights):
    tenants, ranks = mask.shape[1], rank.shape[1]
    parts = []
    for at, size in pieces(tenants * ranks):
        low, high = at // ranks, (at + size) // ranks
        grad = dot(spread(rank, mask[:, low:high]), rows, CONTRACT_ROWS)
        parts.append(grad.reshape(high - low, ranks, -1) * weights[low:high, None, None])
    return jnp.concatenate(parts, axis=0)


def shards(grad_output, hidden, down_weight, adapter_down, adapter_up, job_tenant, job_count):
    index = lax.axis_index("seq")
    group = lax.axis_index("grp")
    count = lax.axis_size("seq")
    groups = lax.axis_size("grp")
    chips = count // CORES
    chip, core = index // CORES, index % CORES
    block = grad_output.shape[0]
    tenants, ranks, down_slab = adapter_down.shape
    up_slab = adapter_up.shape[2]
    width = down_weight.shape[0]
    part = block // groups

    named = (job_tenant[:, :, None] == jnp.arange(tenants, dtype=jnp.int32)).astype(jnp.float32)
    totals = jnp.sum(job_count.astype(jnp.float32)[:, :, None] * named, axis=(0, 1))
    weights = ADAPTER_SCALE / totals
    ends = jnp.cumsum(job_count, axis=1)
    places = jnp.arange(block, dtype=jnp.int32)[None, :, None]
    member = (places >= (ends - job_count)[:, None, :]) & (places < ends[:, None, :])
    owner = jnp.sum(jnp.where(member, job_tenant[:, None, :], 0), axis=2).reshape(count * block)
    mask = (owner[:, None] == jnp.arange(tenants, dtype=jnp.int32)).astype(jnp.float32)

    def seq_move(value, chips_back, flip):
        pairs = [
            (s, ((s // CORES - chips_back) % chips) * CORES + ((s % CORES) ^ flip))
            for s in range(count)
        ]
        return lax.ppermute(value, "seq", pairs)

    def grp_move(value, flip):
        return lax.ppermute(value, "grp", [(g, g ^ flip) for g in range(groups)])

    hidden_slab = lax.all_to_all(
        hidden.reshape(block, count, down_slab).transpose(1, 0, 2),
        "seq",
        split_axis=0,
        concat_axis=0,
        tiled=True,
    ).reshape(count * block, down_slab)

    held = grad_output
    slabs = []
    arrived = []
    for step in range(chips):
        if step:
            held = seq_move(held, -1, 0)
        both = jnp.stack([held, seq_move(held, 0, 1)])
        slabs.append(lax.dynamic_slice_in_dim(both, index * up_slab, up_slab, 2))
        partial = (
            dot(both.reshape(CORES * block, -1), down_weight, CONTRACT_LAST)
            .astype(jnp.bfloat16)
            .reshape(CORES, groups, part, width)
        )
        total = lax.dynamic_index_in_dim(partial, group, 1, keepdims=False).astype(jnp.float32)
        for flip in range(1, groups):
            sent = lax.dynamic_index_in_dim(partial, group ^ flip, 1, keepdims=False)
            total = total + grp_move(sent, flip).astype(jnp.float32)
        total = total.astype(jnp.bfloat16)
        arrived.append(
            jnp.stack(
                [
                    total[flip] if step == 0 and flip == 0 else seq_move(total[flip], step, flip)
                    for flip in range(CORES)
                ]
            )
        )

    places_of = jnp.arange(count, dtype=jnp.int32)
    flips = (places_of % CORES) ^ core
    back = ((chip - places_of // CORES) % chips) * CORES + flips
    ahead = ((places_of // CORES - chip) % chips) * CORES + flips
    grad_slab = jnp.take(jnp.stack(slabs).reshape(count, block, up_slab), back, axis=0)
    grad_slab = grad_slab.reshape(count * block, up_slab)
    base = jnp.take(jnp.stack(arrived).reshape(count, part, width), ahead, axis=0)
    base = lax.all_to_all(base, "grp", split_axis=0, concat_axis=0, tiled=True)
    base = base.reshape(groups, count // groups, part, width).transpose(0, 2, 1, 3)
    base = base.reshape(block, -1)

    grad_rank = lax.psum(project(grad_slab, adapter_up, mask), ("grp", "seq"))
    own_slab, grad_rank = lax.optimization_barrier((hidden_slab, grad_rank))
    act_rank = lax.psum(project(own_slab, adapter_down, mask), ("grp", "seq"))

    flat_down = adapter_down.reshape(tenants * ranks, down_slab)
    term = jnp.concatenate(
        [
            jnp.dot(
                spread(grad_rank[at : at + size], mask[at : at + size]),
                flat_down,
                preferred_element_type=jnp.float32,
            )
            for at, size in pieces(count * block)
        ],
        axis=0,
    )
    term = (term * ADAPTER_SCALE).astype(jnp.bfloat16).reshape(count, block, down_slab)
    term = lax.all_to_all(term, "seq", split_axis=0, concat_axis=0, tiled=True)
    term = term.transpose(1, 0, 2).reshape(block, -1)
    grad_hidden = (base.astype(jnp.float32) + term.astype(jnp.float32)).astype(jnp.bfloat16)

    grad_down = adapter_grad(grad_rank, mask, hidden_slab, weights)
    grad_up = adapter_grad(act_rank, mask, grad_slab, weights)
    return grad_hidden, grad_down, grad_up


def solution(mesh):
    placed = (
        P("seq", "grp"),
        P("seq", "grp"),
        P("seq", "grp"),
        P(None, None, ("grp", "seq")),
        P(None, None, ("grp", "seq")),
        P(),
        P(),
    )
    return jax.shard_map(
        shards,
        mesh=mesh,
        in_specs=placed,
        out_specs=(P("seq", "grp"), P(None, None, ("grp", "seq")), P(None, None, ("grp", "seq"))),
        check_vma=False,
    )
```

```python
import functools

import jax
import jax.numpy as jnp
from jax import lax
from jax.experimental import pallas as pl
from jax.experimental.pallas import tpu as pltpu
from jax.sharding import PartitionSpec as P

ADAPTER_SCALE = 2.0
CONTRACT_LAST = (((1,), (1,)), ((), ()))
CONTRACT_ROWS = (((0,), (0,)), ((), ()))
CORES = 2
MOST_ROWS = 1024


def dot(left, right, dims):
    return lax.dot_general(left, right, dims, preferred_element_type=jnp.float32)


def pieces(total):
    step = min(total, MOST_ROWS)
    return [(at, min(step, total - at)) for at in range(0, total, step)]


def tile_of(width):
    return next(tile for tile in (512, 448, 384, 256, 128, width) if width % tile == 0 and tile % 128 == 0 or tile == width)


def chunk_kernel(groups, group_ref, near_ref, far_ref, weight_ref, *rest):
    outs, rows = rest[:groups], rest[groups]
    part = near_ref.shape[0] // groups

    @pl.when(pl.program_id(0) == 0)
    def _():
        for flip in range(groups):
            at = pl.multiple_of((group_ref[0] ^ flip) * part, part)
            low = flip * CORES * part
            rows[low : low + part] = near_ref[pl.ds(at, part)]
            rows[low + part : low + 2 * part] = far_ref[pl.ds(at, part)]

    full = dot(rows[...], weight_ref[...], CONTRACT_LAST).astype(jnp.bfloat16)
    for flip in range(groups):
        for core in range(CORES):
            low = (flip * CORES + core) * part
            outs[flip][core] = full[low : low + part]


def chunk_product(near, far, weight, group, groups):
    block, depth = near.shape
    width = weight.shape[0]
    tile = tile_of(width)
    part = block // groups
    return pl.pallas_call(
        functools.partial(chunk_kernel, groups),
        grid_spec=pltpu.PrefetchScalarGridSpec(
            num_scalar_prefetch=1,
            grid=(width // tile,),
            in_specs=[
                pl.BlockSpec((block, depth), lambda at, group: (0, 0)),
                pl.BlockSpec((block, depth), lambda at, group: (0, 0)),
                pl.BlockSpec((tile, depth), lambda at, group: (at, 0)),
            ],
            out_specs=[pl.BlockSpec((CORES, part, tile), lambda at, group: (0, 0, at))] * groups,
            scratch_shapes=[pltpu.VMEM((CORES * block, depth), jnp.bfloat16)],
        ),
        out_shape=[jax.ShapeDtypeStruct((CORES, part, width), jnp.bfloat16)] * groups,
        compiler_params=pltpu.CompilerParams(vmem_limit_bytes=24 << 20),
        cost_estimate=pl.CostEstimate(
            flops=2 * CORES * block * depth * width,
            bytes_accessed=2 * (width * depth + CORES * block * (depth + width)),
            transcendentals=0,
        ),
    )(group.reshape(1), near, far, weight)


def project(rows, adapter, mask):
    tenants, ranks, width = adapter.shape
    flat = adapter.reshape(tenants * ranks, width)
    parts = []
    for at, size in pieces(rows.shape[0]):
        full = dot(rows[at : at + size], flat, CONTRACT_LAST)
        chosen = full.reshape(size, tenants, ranks) * mask[at : at + size, :, None]
        parts.append(jnp.sum(chosen, axis=1))
    return jnp.concatenate(parts, axis=0).astype(jnp.bfloat16)


def spread(rank, mask):
    wide = rank[:, None, :] * mask.astype(jnp.bfloat16)[:, :, None]
    return wide.reshape(rank.shape[0], -1)


def adapter_grad(rank, mask, rows, weights):
    tenants, ranks = mask.shape[1], rank.shape[1]
    parts = []
    for at, size in pieces(tenants * ranks):
        low, high = at // ranks, (at + size) // ranks
        grad = dot(spread(rank, mask[:, low:high]), rows, CONTRACT_ROWS)
        parts.append(grad.reshape(high - low, ranks, -1) * weights[low:high, None, None])
    return jnp.concatenate(parts, axis=0)


def shards(grad_output, hidden, down_weight, adapter_down, adapter_up, job_tenant, job_count):
    index = lax.axis_index("seq")
    group = lax.axis_index("grp")
    count = lax.axis_size("seq")
    groups = lax.axis_size("grp")
    chips = count // CORES
    chip, core = index // CORES, index % CORES
    block = grad_output.shape[0]
    tenants, ranks, down_slab = adapter_down.shape
    up_slab = adapter_up.shape[2]
    width = down_weight.shape[0]
    part = block // groups

    named = (job_tenant[:, :, None] == jnp.arange(tenants, dtype=jnp.int32)).astype(jnp.float32)
    totals = jnp.sum(job_count.astype(jnp.float32)[:, :, None] * named, axis=(0, 1))
    weights = ADAPTER_SCALE / totals
    ends = jnp.cumsum(job_count, axis=1)
    places = jnp.arange(block, dtype=jnp.int32)[None, :, None]
    member = (places >= (ends - job_count)[:, None, :]) & (places < ends[:, None, :])
    owner = jnp.sum(jnp.where(member, job_tenant[:, None, :], 0), axis=2).reshape(count * block)
    mask = (owner[:, None] == jnp.arange(tenants, dtype=jnp.int32)).astype(jnp.float32)

    def seq_move(value, chips_back, flip):
        pairs = [
            (s, ((s // CORES - chips_back) % chips) * CORES + ((s % CORES) ^ flip))
            for s in range(count)
        ]
        return lax.ppermute(value, "seq", pairs)

    def grp_move(value, flip):
        return lax.ppermute(value, "grp", [(g, g ^ flip) for g in range(groups)])

    hidden_slab = lax.all_to_all(
        hidden.reshape(block, count, down_slab).transpose(1, 0, 2),
        "seq",
        split_axis=0,
        concat_axis=0,
        tiled=True,
    ).reshape(count * block, down_slab)

    held = grad_output
    grad_slab = jnp.zeros((count, block, up_slab), jnp.bfloat16)
    arrived = jnp.zeros((count, part, width), jnp.bfloat16)
    for step in range(chips):
        if step:
            held = seq_move(held, -1, 0)
        other = seq_move(held, 0, 1)
        back = ((chip - step) % chips) * CORES
        ahead = ((chip + step) % chips) * CORES
        for flip, rows in enumerate((held, other)):
            columns = lax.dynamic_slice_in_dim(rows, index * up_slab, up_slab, 1)
            grad_slab = lax.dynamic_update_index_in_dim(grad_slab, columns, back + (core ^ flip), 0)
        sent = chunk_product(held, other, down_weight, group, groups)
        total = sent[0].astype(jnp.float32)
        for flip in range(1, groups):
            total = total + grp_move(sent[flip], flip).astype(jnp.float32)
        total = total.astype(jnp.bfloat16)
        for flip in range(CORES):
            came = total[flip] if step == 0 and flip == 0 else seq_move(total[flip], step, flip)
            arrived = lax.dynamic_update_index_in_dim(arrived, came, ahead + (core ^ flip), 0)
    grad_slab = grad_slab.reshape(count * block, up_slab)

    each = count // groups
    columns_of = [
        lax.dynamic_slice_in_dim(arrived, (group ^ flip) * each, each, 0) for flip in range(groups)
    ]
    base = jnp.zeros((groups, part, each, width), jnp.bfloat16)
    for flip in range(groups):
        came = columns_of[flip] if flip == 0 else grp_move(columns_of[flip], flip)
        base = lax.dynamic_update_index_in_dim(base, came.transpose(1, 0, 2), group ^ flip, 0)
    base = base.reshape(block, -1)

    ranked = jnp.concatenate(
        [project(grad_slab, adapter_up, mask), project(hidden_slab, adapter_down, mask)], axis=1
    )
    devices = count * groups
    share = lax.all_to_all(
        ranked.reshape(devices, -1, 2 * ranks),
        ("grp", "seq"),
        split_axis=0,
        concat_axis=0,
        tiled=True,
    )
    share = jnp.sum(share.astype(jnp.float32), axis=0).astype(jnp.bfloat16)
    ranked = lax.all_to_all(
        jnp.broadcast_to(share[None], (devices,) + share.shape),
        ("grp", "seq"),
        split_axis=0,
        concat_axis=0,
        tiled=True,
    ).reshape(count * block, 2 * ranks)
    grad_rank, act_rank = ranked[:, :ranks], ranked[:, ranks:]

    flat_down = adapter_down.reshape(tenants * ranks, down_slab)
    term = jnp.concatenate(
        [
            jnp.dot(
                spread(grad_rank[at : at + size], mask[at : at + size]),
                flat_down,
                preferred_element_type=jnp.float32,
            )
            for at, size in pieces(count * block)
        ],
        axis=0,
    )
    term = (term * ADAPTER_SCALE).astype(jnp.bfloat16).reshape(count, block, down_slab)
    term = lax.all_to_all(term, "seq", split_axis=0, concat_axis=0, tiled=True)
    term = term.transpose(1, 0, 2).reshape(block, -1)
    grad_hidden = (base.astype(jnp.float32) + term.astype(jnp.float32)).astype(jnp.bfloat16)

    grad_down = adapter_grad(grad_rank, mask, hidden_slab, weights)
    grad_up = adapter_grad(act_rank, mask, grad_slab, weights)
    return grad_hidden, grad_down, grad_up


def solution(mesh):
    placed = (
        P("seq", "grp"),
        P("seq", "grp"),
        P("seq", "grp"),
        P(None, None, ("grp", "seq")),
        P(None, None, ("grp", "seq")),
        P(),
        P(),
    )
    return jax.shard_map(
        shards,
        mesh=mesh,
        in_specs=placed,
        out_specs=(P("seq", "grp"), P(None, None, ("grp", "seq")), P(None, None, ("grp", "seq"))),
        check_vma=False,
    )
```

```python
import functools

import jax
import jax.numpy as jnp
from jax import lax
from jax.experimental import pallas as pl
from jax.experimental.pallas import tpu as pltpu
from jax.sharding import PartitionSpec as P

ADAPTER_SCALE = 2.0
CONTRACT_LAST = (((1,), (1,)), ((), ()))
CONTRACT_ROWS = (((0,), (0,)), ((), ()))
CORES = 2
MOST_ROWS = 1024


def dot(left, right, dims):
    return lax.dot_general(left, right, dims, preferred_element_type=jnp.float32)


def pieces(total):
    step = min(total, MOST_ROWS)
    return [(at, min(step, total - at)) for at in range(0, total, step)]


def tile_of(width):
    fits = [tile for tile in (512, 448, 384, 256, 128) if width % tile == 0 and tile % 128 == 0]
    return fits[0] if fits else width


def chunk_kernel(stages, place_ref, near_ref, far_ref, weight_ref, *rest):
    outs, rows = rest[:-1], rest[-1]
    part = near_ref.shape[0] // (2 * len(stages))
    sides = [(ref, flips) for ref, order in zip((near_ref, far_ref), stages) for flips in order]
    cuts = [(ref, flip) for ref, flips in sides for flip in flips]

    @pl.when(pl.program_id(0) == 0)
    def _():
        for at, (ref, flip) in enumerate(cuts):
            low = pl.multiple_of((place_ref[0] ^ flip) * part, part)
            rows[at * part : (at + 1) * part] = ref[pl.ds(low, part)]

    full = dot(rows[...], weight_ref[...], CONTRACT_LAST).astype(jnp.bfloat16)
    for at in range(len(cuts)):
        outs[at // 2][at % 2] = full[at * part : (at + 1) * part]


STAGES = (((0, 2), (1, 3)), ((0, 1), (2, 3)))


def chunk_product(near, far, weight, group):
    block, depth = near.shape
    width = weight.shape[0]
    tile = tile_of(width)
    part = block // (2 * len(STAGES))
    return pl.pallas_call(
        functools.partial(chunk_kernel, STAGES),
        grid_spec=pltpu.PrefetchScalarGridSpec(
            num_scalar_prefetch=1,
            grid=(width // tile,),
            in_specs=[
                pl.BlockSpec((block, depth), lambda at, place: (0, 0)),
                pl.BlockSpec((block, depth), lambda at, place: (0, 0)),
                pl.BlockSpec((tile, depth), lambda at, place: (at, 0)),
            ],
            out_specs=[pl.BlockSpec((2, part, tile), lambda at, place: (0, 0, at))] * 4,
            scratch_shapes=[pltpu.VMEM((CORES * block, depth), jnp.bfloat16)],
        ),
        out_shape=[jax.ShapeDtypeStruct((2, part, width), jnp.bfloat16)] * 4,
        compiler_params=pltpu.CompilerParams(vmem_limit_bytes=24 << 20),
        cost_estimate=pl.CostEstimate(
            flops=2 * CORES * block * depth * width,
            bytes_accessed=2 * (width * depth + CORES * block * (depth + width)),
            transcendentals=0,
        ),
    )(group.reshape(1), near, far, weight)


def join_kernel(groups, slab, place_ref, *refs):
    bases, term_ref, out_ref = refs[:groups], refs[groups], refs[groups + 1]
    width = bases[0].shape[2]
    for flip in range(groups):

        @pl.when(pl.program_id(0) == flip)
        def _():
            for at in range(term_ref.shape[0]):
                low = at * slab
                base = bases[flip][low // width, :, low % width : low % width + slab]
                total = base.astype(jnp.float32) + term_ref[at].astype(jnp.float32)
                out_ref[:, low : low + slab] = total.astype(jnp.bfloat16)


def join(bases, term, group):
    groups = len(bases)
    each, part, width = bases[0].shape
    count, block, slab = term.shape
    if slab % 128:
        base = jnp.zeros((groups, part, each, width), jnp.bfloat16)
        for flip, rows in enumerate(bases):
            base = lax.dynamic_update_index_in_dim(base, rows.transpose(1, 0, 2), group ^ flip, 0)
        total = base.reshape(block, -1).astype(jnp.float32)
        return (total + term.transpose(1, 0, 2).reshape(block, -1)).astype(jnp.bfloat16)
    return pl.pallas_call(
        functools.partial(join_kernel, groups, slab),
        grid_spec=pltpu.PrefetchScalarGridSpec(
            num_scalar_prefetch=1,
            grid=(groups,),
            in_specs=[pl.BlockSpec((each, part, width), lambda at, place: (0, 0, 0))] * groups
            + [pl.BlockSpec((count, part, slab), lambda at, place: (0, place[0] ^ at, 0))],
            out_specs=pl.BlockSpec((part, each * width), lambda at, place: (place[0] ^ at, 0)),
        ),
        out_shape=jax.ShapeDtypeStruct((block, each * width), jnp.bfloat16),
        cost_estimate=pl.CostEstimate(
            flops=block * each * width, bytes_accessed=6 * block * each * width, transcendentals=0
        ),
    )(group.reshape(1), *bases, term)


def add(*terms):
    return sum(term.astype(jnp.float32) for term in terms).astype(jnp.bfloat16)


def after(value, *others):
    return lax.optimization_barrier((value,) + others)[0]


def project(rows, adapter, mask):
    tenants, ranks, width = adapter.shape
    flat = adapter.reshape(tenants * ranks, width)
    parts = []
    for at, size in pieces(rows.shape[0]):
        full = dot(rows[at : at + size], flat, CONTRACT_LAST)
        chosen = full.reshape(size, tenants, ranks) * mask[at : at + size, :, None]
        parts.append(jnp.sum(chosen, axis=1))
    return jnp.concatenate(parts, axis=0).astype(jnp.bfloat16)


def spread(rank, mask):
    wide = rank[:, None, :] * mask.astype(jnp.bfloat16)[:, :, None]
    return wide.reshape(rank.shape[0], -1)


def adapter_grad(rank, mask, rows, weights):
    tenants, ranks = mask.shape[1], rank.shape[1]
    parts = []
    for at, size in pieces(tenants * ranks):
        low, high = at // ranks, (at + size) // ranks
        grad = dot(spread(rank, mask[:, low:high]), rows, CONTRACT_ROWS)
        parts.append(grad.reshape(high - low, ranks, -1) * weights[low:high, None, None])
    return jnp.concatenate(parts, axis=0)


def shards(grad_output, hidden, down_weight, adapter_down, adapter_up, job_tenant, job_count):
    index = lax.axis_index("seq")
    group = lax.axis_index("grp")
    count = lax.axis_size("seq")
    groups = lax.axis_size("grp")
    chips = count // CORES
    chip, core = index // CORES, index % CORES
    block = grad_output.shape[0]
    tenants, ranks, down_slab = adapter_down.shape
    up_slab = adapter_up.shape[2]
    width = down_weight.shape[0]
    part = block // groups

    named = (job_tenant[:, :, None] == jnp.arange(tenants, dtype=jnp.int32)).astype(jnp.float32)
    totals = jnp.sum(job_count.astype(jnp.float32)[:, :, None] * named, axis=(0, 1))
    weights = ADAPTER_SCALE / totals
    ends = jnp.cumsum(job_count, axis=1)
    places = jnp.arange(block, dtype=jnp.int32)[None, :, None]
    member = (places >= (ends - job_count)[:, None, :]) & (places < ends[:, None, :])
    owner = jnp.sum(jnp.where(member, job_tenant[:, None, :], 0), axis=2).reshape(count * block)
    mask = (owner[:, None] == jnp.arange(tenants, dtype=jnp.int32)).astype(jnp.float32)

    def seq_move(value, chips_back, flip):
        pairs = [
            (s, ((s // CORES - chips_back) % chips) * CORES + ((s % CORES) ^ flip))
            for s in range(count)
        ]
        return lax.ppermute(value, "seq", pairs)

    def grp_move(value, flip):
        return lax.ppermute(value, "grp", [(g, g ^ flip) for g in range(groups)])

    held = [grad_output]
    for step in range(1, chips):
        held.append(seq_move(held[-1], -1, 0))
    pairs = [(near, seq_move(near, 0, 1)) for near in held]

    hidden_slab = lax.all_to_all(
        hidden.reshape(block, count, down_slab).transpose(1, 0, 2),
        "seq",
        split_axis=0,
        concat_axis=0,
        tiled=True,
    ).reshape(count * block, down_slab)

    last = chips - 1
    products = [chunk_product(near, far, down_weight, group) for near, far in pairs]
    firsts = [
        (grp_move(near_sent, 1), grp_move(far_sent, 2)) for _, near_sent, _, far_sent in products
    ]
    grad_slab = jnp.zeros((count, block, up_slab), jnp.bfloat16)
    for step, pair in enumerate(pairs):
        back = ((chip - step) % chips) * CORES
        for flip, rows in enumerate(pair):
            columns = lax.dynamic_slice_in_dim(rows, index * up_slab, up_slab, 1)
            grad_slab = lax.dynamic_update_index_in_dim(grad_slab, columns, back + (core ^ flip), 0)
    grad_slab = grad_slab.reshape(count * block, up_slab)

    def second(step, *gates):
        near_kept, _, far_kept, _ = products[step]
        near_came, far_came = firsts[step]
        near_came, far_came = lax.optimization_barrier((near_came, far_came) + gates)[:2]
        near_sum = add(near_kept[1], near_came[1])
        far_sum = add(far_kept[1], far_came[1])
        return near_sum, (grp_move(near_sum, 2), grp_move(far_sum, 1))

    def total(step, seconds, *gates):
        near_kept, _, far_kept, _ = products[step]
        near_came, far_came = firsts[step]
        near_last, far_last = lax.optimization_barrier(seconds + gates)[:2]
        return (
            add(near_kept[0], near_came[0], near_last),
            add(far_kept[0], far_came[0], far_last),
        )

    arrived = jnp.zeros((count, part, width), jnp.bfloat16)

    def hop(step, sums):
        return [
            sums[flip] if step == 0 and flip == 0 else seq_move(sums[flip], step, flip)
            for flip in range(CORES)
        ]

    def put(arrived, step, came, *gates):
        ahead = ((chip + step) % chips) * CORES
        came = lax.optimization_barrier(tuple(came) + gates)
        for flip in range(CORES):
            arrived = lax.dynamic_update_index_in_dim(arrived, came[flip], ahead + (core ^ flip), 0)
        return arrived

    came = None
    for step in range(last - 1):
        _, seconds = second(step, products[step + 1][0])
        sums = total(step, seconds)
        if came is not None:
            arrived = put(arrived, step - 1, came, sums[0])
        came = hop(step, sums)

    begun, seconds = second(last - 1, products[last][0])
    rows_here = lax.optimization_barrier((grad_slab, hidden_slab, begun))
    ranked = jnp.concatenate(
        [project(rows_here[0], adapter_up, mask), project(rows_here[1], adapter_down, mask)],
        axis=1,
    )
    devices = count * groups
    share = lax.all_to_all(
        ranked.reshape(devices, -1, 2 * ranks),
        ("grp", "seq"),
        split_axis=0,
        concat_axis=0,
        tiled=True,
    )
    sums = total(last - 1, seconds, ranked)
    arrived = put(arrived, last - 2, came, sums[0])
    came = hop(last - 1, sums)
    begun, seconds = second(last, sums[0])
    share = after(share, begun)
    share = jnp.sum(share.astype(jnp.float32), axis=0).astype(jnp.bfloat16)
    ranked = lax.all_to_all(
        jnp.broadcast_to(share[None], (devices,) + share.shape),
        ("grp", "seq"),
        split_axis=0,
        concat_axis=0,
        tiled=True,
    ).reshape(count * block, 2 * ranks)
    sums = total(last, seconds, share)
    arrived = put(arrived, last - 1, came, sums[0])
    came = hop(last, sums)
    ranked = after(ranked, *sums)
    grad_rank = ranked[:, :ranks]

    flat_down = adapter_down.reshape(tenants * ranks, down_slab)
    term = jnp.concatenate(
        [
            jnp.dot(
                spread(grad_rank[at : at + size], mask[at : at + size]),
                flat_down,
                preferred_element_type=jnp.float32,
            )
            for at, size in pieces(count * block)
        ],
        axis=0,
    )
    term = (term * ADAPTER_SCALE).astype(jnp.bfloat16).reshape(count, block, down_slab)
    arrived = put(arrived, last, came, term)
    rank_here = after(ranked, term)
    term = lax.all_to_all(term, "seq", split_axis=0, concat_axis=0, tiled=True)

    each = count // groups
    bases = []
    for flip in range(groups):
        sums = lax.dynamic_slice_in_dim(arrived, (group ^ flip) * each, each, 0)
        bases.append(grp_move(sums, flip) if flip else sums)

    grad_down = adapter_grad(rank_here[:, :ranks], mask, hidden_slab, weights)
    grad_up = adapter_grad(rank_here[:, ranks:], mask, grad_slab, weights)
    grad_hidden = join(bases, term, group)
    return grad_hidden, grad_down, grad_up


def solution(mesh):
    placed = (
        P("seq", "grp"),
        P("seq", "grp"),
        P("seq", "grp"),
        P(None, None, ("grp", "seq")),
        P(None, None, ("grp", "seq")),
        P(),
        P(),
    )
    return jax.shard_map(
        shards,
        mesh=mesh,
        in_specs=placed,
        out_specs=(P("seq", "grp"), P(None, None, ("grp", "seq")), P(None, None, ("grp", "seq"))),
        check_vma=False,
    )
```

```python
import functools

import jax
import jax.numpy as jnp
from jax import lax
from jax.experimental import pallas as pl
from jax.experimental.pallas import tpu as pltpu
from jax.sharding import PartitionSpec as P

ADAPTER_SCALE = 2.0
CONTRACT_LAST = (((1,), (1,)), ((), ()))
CONTRACT_ROWS = (((0,), (0,)), ((), ()))
CORES = 2
MOST_ROWS = 1024
VMEM_GRANT = 56 << 20


def dot(left, right, dims):
    return lax.dot_general(left, right, dims, preferred_element_type=jnp.float32)


def pieces(total):
    step = min(total, MOST_ROWS)
    return [(at, min(step, total - at)) for at in range(0, total, step)]


def tile_of(width):
    fits = [tile for tile in (512, 448, 384, 256, 128) if width % tile == 0 and tile % 128 == 0]
    return fits[0] if fits else width


def chunk_kernel(stages, place_ref, near_ref, far_ref, weight_ref, *rest):
    outs, rows = rest[:-1], rest[-1]
    part = near_ref.shape[0] // (2 * len(stages))
    sides = [(ref, flips) for ref, order in zip((near_ref, far_ref), stages) for flips in order]
    cuts = [(ref, flip) for ref, flips in sides for flip in flips]

    @pl.when(pl.program_id(0) == 0)
    def _():
        for at, (ref, flip) in enumerate(cuts):
            low = pl.multiple_of((place_ref[0] ^ flip) * part, part)
            rows[at * part : (at + 1) * part] = ref[pl.ds(low, part)]

    full = dot(rows[...], weight_ref[...], CONTRACT_LAST).astype(jnp.bfloat16)
    for at in range(len(cuts)):
        outs[at // 2][at % 2] = full[at * part : (at + 1) * part]


STAGES = (((0, 2), (1, 3)), ((0, 1), (2, 3)))


def chunk_product(near, far, weight, group):
    block, depth = near.shape
    width = weight.shape[0]
    tile = tile_of(width)
    part = block // (2 * len(STAGES))
    return pl.pallas_call(
        functools.partial(chunk_kernel, STAGES),
        grid_spec=pltpu.PrefetchScalarGridSpec(
            num_scalar_prefetch=1,
            grid=(width // tile,),
            in_specs=[
                pl.BlockSpec((block, depth), lambda at, place: (0, 0)),
                pl.BlockSpec((block, depth), lambda at, place: (0, 0)),
                pl.BlockSpec((tile, depth), lambda at, place: (at, 0)),
            ],
            out_specs=[pl.BlockSpec((2, part, tile), lambda at, place: (0, 0, at))] * 4,
            scratch_shapes=[pltpu.VMEM((CORES * block, depth), jnp.bfloat16)],
        ),
        out_shape=[jax.ShapeDtypeStruct((2, part, width), jnp.bfloat16)] * 4,
        compiler_params=pltpu.CompilerParams(vmem_limit_bytes=VMEM_GRANT),
        cost_estimate=pl.CostEstimate(
            flops=2 * CORES * block * depth * width,
            bytes_accessed=2 * (width * depth + CORES * block * (depth + width)),
            transcendentals=0,
        ),
    )(group.reshape(1), near, far, weight)


def join_kernel(groups, slab, place_ref, *refs):
    bases, term_ref, out_ref = refs[:groups], refs[groups], refs[groups + 1]
    width = bases[0].shape[2]
    for flip in range(groups):

        @pl.when(pl.program_id(0) == flip)
        def _():
            for at in range(term_ref.shape[0]):
                low = at * slab
                base = bases[flip][low // width, :, low % width : low % width + slab]
                total = base.astype(jnp.float32) + term_ref[at].astype(jnp.float32)
                out_ref[:, low : low + slab] = total.astype(jnp.bfloat16)


def join(bases, term, group):
    groups = len(bases)
    each, part, width = bases[0].shape
    count, block, slab = term.shape
    if slab % 128:
        base = jnp.zeros((groups, part, each, width), jnp.bfloat16)
        for flip, rows in enumerate(bases):
            base = lax.dynamic_update_index_in_dim(base, rows.transpose(1, 0, 2), group ^ flip, 0)
        total = base.reshape(block, -1).astype(jnp.float32)
        return (total + term.transpose(1, 0, 2).reshape(block, -1)).astype(jnp.bfloat16)
    return pl.pallas_call(
        functools.partial(join_kernel, groups, slab),
        grid_spec=pltpu.PrefetchScalarGridSpec(
            num_scalar_prefetch=1,
            grid=(groups,),
            in_specs=[pl.BlockSpec((each, part, width), lambda at, place: (0, 0, 0))] * groups
            + [pl.BlockSpec((count, part, slab), lambda at, place: (0, place[0] ^ at, 0))],
            out_specs=pl.BlockSpec((part, each * width), lambda at, place: (place[0] ^ at, 0)),
        ),
        out_shape=jax.ShapeDtypeStruct((block, each * width), jnp.bfloat16),
        cost_estimate=pl.CostEstimate(
            flops=block * each * width, bytes_accessed=6 * block * each * width, transcendentals=0
        ),
    )(group.reshape(1), *bases, term)


ANYWHERE = pl.BlockSpec(memory_space=pl.ANY)


def touch_kernel(*refs):
    pass


def touch(value, *gates):
    return pl.pallas_call(
        touch_kernel,
        in_specs=[ANYWHERE] * (1 + len(gates)),
        out_specs=ANYWHERE,
        out_shape=jax.ShapeDtypeStruct(value.shape, value.dtype),
        input_output_aliases={0: 0},
    )(value, *gates)


def cut_kernel(rows_ref, out_ref):
    out_ref[0] = rows_ref[...]


def cut_columns(rows, count):
    block, width = rows.shape
    slab = width // count
    if slab % 128:
        return rows.reshape(block, count, slab).transpose(1, 0, 2)
    return pl.pallas_call(
        cut_kernel,
        grid=(count,),
        in_specs=[pl.BlockSpec((block, slab), lambda at: (0, at))],
        out_specs=pl.BlockSpec((1, block, slab), lambda at: (at, 0, 0)),
        out_shape=jax.ShapeDtypeStruct((count, block, slab), rows.dtype),
        cost_estimate=pl.CostEstimate(flops=0, bytes_accessed=4 * rows.size, transcendentals=0),
    )(rows)


def add(*terms):
    return sum(term.astype(jnp.float32) for term in terms).astype(jnp.bfloat16)


def half_kernel(near_kept, near_came, far_kept, far_came, *rest):
    near_out, far_out = rest[-2:]
    near_out[...] = add(near_kept[0], near_came[0])
    far_out[...] = add(far_kept[0], far_came[0])


def half_sums(near_kept, near_came, far_kept, far_came, *gates):
    _, part, width = near_kept.shape
    return pl.pallas_call(
        half_kernel,
        grid=(1,),
        in_specs=[pl.BlockSpec((1, part, width), lambda at: (1, 0, 0))] * 4
        + [ANYWHERE] * len(gates),
        out_specs=[pl.BlockSpec((part, width), lambda at: (0, 0))] * 2,
        out_shape=[jax.ShapeDtypeStruct((part, width), jnp.bfloat16)] * 2,
    )(near_kept, near_came, far_kept, far_came, *gates)


def full_kernel(place_ref, *refs):
    out_ref = refs[-1]
    for side in range(2):

        @pl.when(pl.program_id(0) == side)
        def _():
            kept, came, last = refs[3 * side : 3 * side + 3]
            out_ref[0] = add(kept[0], came[0], last[...])


def full_sums(sides, places, filled, count):
    part, width = sides[0][2].shape
    first = pl.BlockSpec((1, part, width), lambda at, place: (0, 0, 0))
    whole = pl.BlockSpec((part, width), lambda at, place: (0, 0))
    extra = [] if filled is None else [filled]
    return pl.pallas_call(
        full_kernel,
        grid_spec=pltpu.PrefetchScalarGridSpec(
            num_scalar_prefetch=1,
            grid=(2,),
            in_specs=[first, first, whole] * 2 + [ANYWHERE] * len(extra),
            out_specs=pl.BlockSpec((1, part, width), lambda at, place: (place[at], 0, 0)),
        ),
        out_shape=jax.ShapeDtypeStruct((count, part, width), jnp.bfloat16),
        input_output_aliases={7: 0} if extra else {},
    )(jnp.stack(places), *sides[0], *sides[1], *extra)


def project(rows, adapter, mask):
    tenants, ranks, width = adapter.shape
    flat = adapter.reshape(tenants * ranks, width)
    parts = []
    for at, size in pieces(rows.shape[0]):
        full = dot(rows[at : at + size], flat, CONTRACT_LAST)
        chosen = full.reshape(size, tenants, ranks) * mask[at : at + size, :, None]
        parts.append(jnp.sum(chosen, axis=1))
    return jnp.concatenate(parts, axis=0).astype(jnp.bfloat16)


def spread(rank, mask):
    wide = rank[:, None, :] * mask.astype(jnp.bfloat16)[:, :, None]
    return wide.reshape(rank.shape[0], -1)


def adapter_grad(rank, mask, rows, weights):
    tenants, ranks = mask.shape[1], rank.shape[1]
    parts = []
    for at, size in pieces(tenants * ranks):
        low, high = at // ranks, (at + size) // ranks
        grad = dot(spread(rank, mask[:, low:high]), rows, CONTRACT_ROWS)
        parts.append(grad.reshape(high - low, ranks, -1) * weights[low:high, None, None])
    return jnp.concatenate(parts, axis=0)


def shards(grad_output, hidden, down_weight, adapter_down, adapter_up, job_tenant, job_count):
    index = lax.axis_index("seq")
    group = lax.axis_index("grp")
    count = lax.axis_size("seq")
    groups = lax.axis_size("grp")
    chips = count // CORES
    chip, core = index // CORES, index % CORES
    block = grad_output.shape[0]
    tenants, ranks, down_slab = adapter_down.shape
    up_slab = adapter_up.shape[2]
    width = down_weight.shape[0]
    part = block // groups

    named = (job_tenant[:, :, None] == jnp.arange(tenants, dtype=jnp.int32)).astype(jnp.float32)
    totals = jnp.sum(job_count.astype(jnp.float32)[:, :, None] * named, axis=(0, 1))
    weights = ADAPTER_SCALE / totals
    ends = jnp.cumsum(job_count, axis=1)
    places = jnp.arange(block, dtype=jnp.int32)[None, :, None]
    member = (places >= (ends - job_count)[:, None, :]) & (places < ends[:, None, :])
    owner = jnp.sum(jnp.where(member, job_tenant[:, None, :], 0), axis=2).reshape(count * block)
    mask = (owner[:, None] == jnp.arange(tenants, dtype=jnp.int32)).astype(jnp.float32)

    def seq_move(value, chips_back, flip):
        pairs = [
            (s, ((s // CORES - chips_back) % chips) * CORES + ((s % CORES) ^ flip))
            for s in range(count)
        ]
        return lax.ppermute(value, "seq", pairs)

    def grp_move(value, flip):
        return lax.ppermute(value, "grp", [(g, g ^ flip) for g in range(groups)])

    held = [grad_output]
    for step in range(1, chips):
        held.append(seq_move(held[-1], -1, 0))
    pairs = [(near, seq_move(near, 0, 1)) for near in held]

    cut = touch(cut_columns(hidden, count), held[min(2, chips - 1)])
    hidden_slab = lax.all_to_all(cut, "seq", split_axis=0, concat_axis=0, tiled=True)
    hidden_slab = hidden_slab.reshape(count * block, down_slab)

    products = [chunk_product(near, far, down_weight, group) for near, far in pairs]
    firsts = [
        (grp_move(near_sent, 1), grp_move(far_sent, 2)) for _, near_sent, _, far_sent in products
    ]
    summed = None
    for step in range(chips):
        near_kept, _, far_kept, _ = products[step]
        near_came, far_came = firsts[step]
        gates = [products[step + 1][0]] if step + 1 < chips else []
        near_sum, far_sum = half_sums(near_kept, near_came, far_kept, far_came, *gates)
        sides = (
            (near_kept, near_came, grp_move(near_sum, 2)),
            (far_kept, far_came, grp_move(far_sum, 1)),
        )
        back = ((chip - step) % chips) * CORES
        summed = full_sums(sides, (back + core, back + 1 - core), summed, count)

    arrived = lax.all_to_all(summed, "seq", split_axis=0, concat_axis=0, tiled=True)

    grad_slab = jnp.zeros((count, block, up_slab), jnp.bfloat16)
    for step, pair in enumerate(pairs):
        back = ((chip - step) % chips) * CORES
        for flip, rows in enumerate(pair):
            columns = lax.dynamic_slice_in_dim(rows, index * up_slab, up_slab, 1)
            grad_slab = lax.dynamic_update_index_in_dim(grad_slab, columns, back + (core ^ flip), 0)
    grad_slab = touch(grad_slab.reshape(count * block, up_slab), summed)
    hidden_slab = touch(hidden_slab, summed)

    def sum_ranks(parts):
        rows = parts.shape[0] // 2
        parts = jnp.concatenate([parts[:rows], parts[rows:]], axis=1)
        for axis in ("seq", "grp"):
            size = lax.axis_size(axis)
            flip = 1
            while flip < size:
                pairs = [(at, at ^ flip) for at in range(size)]
                parts = add(parts, lax.ppermute(parts, axis, pairs))
                flip *= 2
        return jnp.concatenate([parts[:, :ranks], parts[:, ranks:]], axis=0)

    grad_rank = sum_ranks(project(grad_slab, adapter_up, mask))
    act_rank = sum_ranks(project(hidden_slab, adapter_down, mask))

    flat_down = adapter_down.reshape(tenants * ranks, down_slab)
    term = jnp.concatenate(
        [
            jnp.dot(
                spread(grad_rank[at : at + size], mask[at : at + size]),
                flat_down,
                preferred_element_type=jnp.float32,
            )
            for at, size in pieces(count * block)
        ],
        axis=0,
    )
    term = (term * ADAPTER_SCALE).astype(jnp.bfloat16).reshape(count, block, down_slab)
    term = lax.all_to_all(term, "seq", split_axis=0, concat_axis=0, tiled=True)

    each = count // groups
    bases = []
    for flip in range(groups):
        sums = lax.dynamic_slice_in_dim(arrived, (group ^ flip) * each, each, 0)
        bases.append(grp_move(sums, flip) if flip else sums)

    grad_down = adapter_grad(grad_rank, mask, hidden_slab, weights)
    grad_up = adapter_grad(act_rank, mask, grad_slab, weights)
    grad_hidden = join(bases, term, group)
    return grad_hidden, grad_down, grad_up


def solution(mesh):
    placed = (
        P("seq", "grp"),
        P("seq", "grp"),
        P("seq", "grp"),
        P(None, None, ("grp", "seq")),
        P(None, None, ("grp", "seq")),
        P(),
        P(),
    )
    return jax.shard_map(
        shards,
        mesh=mesh,
        in_specs=placed,
        out_specs=(P("seq", "grp"), P(None, None, ("grp", "seq")), P(None, None, ("grp", "seq"))),
        check_vma=False,
    )
```

```python
import functools

import jax
import jax.numpy as jnp
from jax import lax
from jax.experimental import pallas as pl
from jax.experimental.pallas import tpu as pltpu
from jax.sharding import PartitionSpec as P

ADAPTER_SCALE = 2.0
CONTRACT_LAST = (((1,), (1,)), ((), ()))
CONTRACT_ROWS = (((0,), (0,)), ((), ()))
CORES = 2
MOST_ROWS = 1024
ANYWHERE = pl.BlockSpec(memory_space=pl.ANY)


def dot(left, right, dims):
    return lax.dot_general(left, right, dims, preferred_element_type=jnp.float32)


def pieces(total):
    step = min(total, MOST_ROWS)
    return [(at, min(step, total - at)) for at in range(0, total, step)]


def tile_of(width):
    fits = [tile for tile in (512, 448, 384, 256, 128) if width % tile == 0 and tile % 128 == 0]
    return fits[0] if fits else width


def chunk_kernel(stages, place_ref, near_ref, far_ref, weight_ref, *rest):
    outs, rows = rest[-5:-1], rest[-1]
    part = near_ref.shape[0] // (2 * len(stages))
    sides = [(ref, flips) for ref, order in zip((near_ref, far_ref), stages) for flips in order]
    cuts = [(ref, flip) for ref, flips in sides for flip in flips]

    @pl.when(pl.program_id(0) == 0)
    def _():
        for at, (ref, flip) in enumerate(cuts):
            low = pl.multiple_of((place_ref[0] ^ flip) * part, part)
            rows[at * part : (at + 1) * part] = ref[pl.ds(low, part)]

    full = dot(rows[...], weight_ref[...], CONTRACT_LAST).astype(jnp.bfloat16)
    for at in range(len(cuts)):
        outs[at // 2][at % 2] = full[at * part : (at + 1) * part]


STAGES = (((0, 2), (1, 3)), ((0, 1), (2, 3)))


def chunk_product(near, far, weight, group, *gates):
    block, depth = near.shape
    width = weight.shape[0]
    tile = tile_of(width)
    part = block // (2 * len(STAGES))
    return pl.pallas_call(
        functools.partial(chunk_kernel, STAGES),
        grid_spec=pltpu.PrefetchScalarGridSpec(
            num_scalar_prefetch=1,
            grid=(width // tile,),
            in_specs=[
                pl.BlockSpec((block, depth), lambda at, place: (0, 0)),
                pl.BlockSpec((block, depth), lambda at, place: (0, 0)),
                pl.BlockSpec((tile, depth), lambda at, place: (at, 0)),
            ]
            + [ANYWHERE] * len(gates),
            out_specs=[pl.BlockSpec((2, part, tile), lambda at, place: (0, 0, at))] * 4,
            scratch_shapes=[pltpu.VMEM((CORES * block, depth), jnp.bfloat16)],
        ),
        out_shape=[jax.ShapeDtypeStruct((2, part, width), jnp.bfloat16)] * 4,
        compiler_params=pltpu.CompilerParams(vmem_limit_bytes=24 << 20),
        cost_estimate=pl.CostEstimate(
            flops=2 * CORES * block * depth * width,
            bytes_accessed=2 * (width * depth + CORES * block * (depth + width)),
            transcendentals=0,
        ),
    )(group.reshape(1), near, far, weight, *gates)


def join_kernel(groups, slab, place_ref, *refs):
    bases, term_ref, out_ref = refs[:groups], refs[groups], refs[groups + 1]
    width = bases[0].shape[2]
    for flip in range(groups):

        @pl.when(pl.program_id(0) == flip)
        def _():
            for at in range(term_ref.shape[0]):
                low = at * slab
                base = bases[flip][low // width, :, low % width : low % width + slab]
                total = base.astype(jnp.float32) + term_ref[at].astype(jnp.float32)
                out_ref[:, low : low + slab] = total.astype(jnp.bfloat16)


def join(bases, term, group):
    groups = len(bases)
    each, part, width = bases[0].shape
    count, block, slab = term.shape
    if slab % 128:
        base = jnp.zeros((groups, part, each, width), jnp.bfloat16)
        for flip, rows in enumerate(bases):
            base = lax.dynamic_update_index_in_dim(base, rows.transpose(1, 0, 2), group ^ flip, 0)
        total = base.reshape(block, -1).astype(jnp.float32)
        return (total + term.transpose(1, 0, 2).reshape(block, -1)).astype(jnp.bfloat16)
    return pl.pallas_call(
        functools.partial(join_kernel, groups, slab),
        grid_spec=pltpu.PrefetchScalarGridSpec(
            num_scalar_prefetch=1,
            grid=(groups,),
            in_specs=[pl.BlockSpec((each, part, width), lambda at, place: (0, 0, 0))] * groups
            + [pl.BlockSpec((count, part, slab), lambda at, place: (0, place[0] ^ at, 0))],
            out_specs=pl.BlockSpec((part, each * width), lambda at, place: (place[0] ^ at, 0)),
        ),
        out_shape=jax.ShapeDtypeStruct((block, each * width), jnp.bfloat16),
        cost_estimate=pl.CostEstimate(
            flops=block * each * width, bytes_accessed=6 * block * each * width, transcendentals=0
        ),
    )(group.reshape(1), *bases, term)


def add(*terms):
    return sum(term.astype(jnp.float32) for term in terms).astype(jnp.bfloat16)


def touch_kernel(*refs):
    pass


def touch(values, *gates):
    return pl.pallas_call(
        touch_kernel,
        in_specs=[ANYWHERE] * (len(values) + len(gates)),
        out_specs=[ANYWHERE] * len(values),
        out_shape=[jax.ShapeDtypeStruct(value.shape, value.dtype) for value in values],
        input_output_aliases={at: at for at in range(len(values))},
    )(*values, *gates)


def project(rows, adapter, mask):
    tenants, ranks, width = adapter.shape
    flat = adapter.reshape(tenants * ranks, width)
    parts = []
    for at, size in pieces(rows.shape[0]):
        full = dot(rows[at : at + size], flat, CONTRACT_LAST)
        chosen = full.reshape(size, tenants, ranks) * mask[at : at + size, :, None]
        parts.append(jnp.sum(chosen, axis=1))
    return jnp.concatenate(parts, axis=0).astype(jnp.bfloat16)


def spread(rank, mask):
    wide = rank[:, None, :] * mask.astype(jnp.bfloat16)[:, :, None]
    return wide.reshape(rank.shape[0], -1)


def adapter_grad(rank, mask, rows, weights):
    tenants, ranks = mask.shape[1], rank.shape[1]
    parts = []
    for at, size in pieces(tenants * ranks):
        low, high = at // ranks, (at + size) // ranks
        grad = dot(spread(rank, mask[:, low:high]), rows, CONTRACT_ROWS)
        parts.append(grad.reshape(high - low, ranks, -1) * weights[low:high, None, None])
    return jnp.concatenate(parts, axis=0)


def shards(grad_output, hidden, down_weight, adapter_down, adapter_up, job_tenant, job_count):
    index = lax.axis_index("seq")
    group = lax.axis_index("grp")
    count = lax.axis_size("seq")
    groups = lax.axis_size("grp")
    chips = count // CORES
    chip, core = index // CORES, index % CORES
    block = grad_output.shape[0]
    tenants, ranks, down_slab = adapter_down.shape
    up_slab = adapter_up.shape[2]
    width = down_weight.shape[0]
    part = block // groups

    named = (job_tenant[:, :, None] == jnp.arange(tenants, dtype=jnp.int32)).astype(jnp.float32)
    totals = jnp.sum(job_count.astype(jnp.float32)[:, :, None] * named, axis=(0, 1))
    weights = ADAPTER_SCALE / totals
    ends = jnp.cumsum(job_count, axis=1)
    places = jnp.arange(block, dtype=jnp.int32)[None, :, None]
    member = (places >= (ends - job_count)[:, None, :]) & (places < ends[:, None, :])
    owner = jnp.sum(jnp.where(member, job_tenant[:, None, :], 0), axis=2).reshape(count * block)
    mask = (owner[:, None] == jnp.arange(tenants, dtype=jnp.int32)).astype(jnp.float32)

    def seq_move(value, chips_back, flip):
        pairs = [
            (s, ((s // CORES - chips_back) % chips) * CORES + ((s % CORES) ^ flip))
            for s in range(count)
        ]
        return lax.ppermute(value, "seq", pairs)

    def grp_move(value, flip):
        return lax.ppermute(value, "grp", [(g, g ^ flip) for g in range(groups)])

    held = [grad_output]
    for step in range(1, chips):
        held.append(seq_move(held[-1], -1, 0))
    pairs = [(near, seq_move(near, 0, 1)) for near in held]

    hidden_slab = lax.all_to_all(
        hidden.reshape(block, count, down_slab).transpose(1, 0, 2),
        "seq",
        split_axis=0,
        concat_axis=0,
        tiled=True,
    ).reshape(count * block, down_slab)

    last = chips - 1

    def product(step, *gates):
        return chunk_product(*pairs[step], down_weight, group, *gates)

    products = [product(step) for step in range(last - 1)]
    (hidden_slab,) = touch([hidden_slab], products[-1][0])
    grad_slab = jnp.zeros((count, block, up_slab), jnp.bfloat16)
    for step, pair in enumerate(pairs):
        back = ((chip - step) % chips) * CORES
        for flip, rows in enumerate(pair):
            columns = lax.dynamic_slice_in_dim(rows, index * up_slab, up_slab, 1)
            grad_slab = lax.dynamic_update_index_in_dim(grad_slab, columns, back + (core ^ flip), 0)
    grad_slab = grad_slab.reshape(count * block, up_slab)
    act_part = project(hidden_slab, adapter_down, mask)
    grad_part = project(grad_slab, adapter_up, mask)
    ranked = jnp.concatenate([grad_part, act_part], axis=1)

    products += [product(last - 1, act_part), product(last, ranked)]

    firsts = [
        (grp_move(near_sent, 1), grp_move(far_sent, 2)) for _, near_sent, _, far_sent in products
    ]

    def second(step, *gates):
        near_kept, _, far_kept, _ = products[step]
        near_came, far_came = firsts[step] = touch(firsts[step], *gates)
        near_sum = add(near_kept[1], near_came[1])
        far_sum = add(far_kept[1], far_came[1])
        return near_sum, [grp_move(near_sum, 2), grp_move(far_sum, 1)]

    def total(step, seconds, *gates):
        near_kept, _, far_kept, _ = products[step]
        near_came, far_came = firsts[step]
        near_last, far_last = touch(seconds, *gates) if gates else seconds
        return (
            add(near_kept[0], near_came[0], near_last),
            add(far_kept[0], far_came[0], far_last),
        )

    arrived = jnp.zeros((count, part, width), jnp.bfloat16)

    def hop(step, sums):
        return [
            sums[flip] if step == 0 and flip == 0 else seq_move(sums[flip], step, flip)
            for flip in range(CORES)
        ]

    def put(arrived, step, came, *gates):
        ahead = ((chip + step) % chips) * CORES
        came = touch(came, *gates)
        for flip in range(CORES):
            arrived = lax.dynamic_update_index_in_dim(arrived, came[flip], ahead + (core ^ flip), 0)
        return arrived

    came = None
    for step in range(last - 1):
        _, seconds = second(step, products[step + 1][0])
        sums = total(step, seconds)
        if came is not None:
            arrived = put(arrived, step - 1, came, sums[0])
        came = hop(step, sums)

    devices = count * groups
    share = lax.all_to_all(
        ranked.reshape(devices, -1, 2 * ranks),
        ("grp", "seq"),
        split_axis=0,
        concat_axis=0,
        tiled=True,
    )
    begun, seconds = second(last - 1, products[last][0])
    (share,) = touch([share], begun)
    share = jnp.sum(share.astype(jnp.float32), axis=0).astype(jnp.bfloat16)
    ranked = lax.all_to_all(
        jnp.broadcast_to(share[None], (devices,) + share.shape),
        ("grp", "seq"),
        split_axis=0,
        concat_axis=0,
        tiled=True,
    ).reshape(count * block, 2 * ranks)
    sums = total(last - 1, seconds, share)
    arrived = put(arrived, last - 2, came, sums[0])
    came = hop(last - 1, sums)
    _, seconds = second(last, sums[0])
    sums = total(last, seconds)
    arrived = put(arrived, last - 1, came, sums[0])
    came = hop(last, sums)
    (ranked,) = touch([ranked], *sums)
    grad_rank = ranked[:, :ranks]

    flat_down = adapter_down.reshape(tenants * ranks, down_slab)
    term = jnp.concatenate(
        [
            jnp.dot(
                spread(grad_rank[at : at + size], mask[at : at + size]),
                flat_down,
                preferred_element_type=jnp.float32,
            )
            for at, size in pieces(count * block)
        ],
        axis=0,
    )
    term = (term * ADAPTER_SCALE).astype(jnp.bfloat16).reshape(count, block, down_slab)
    arrived = put(arrived, last, came, term)
    (rank_here,) = touch([ranked], term)
    term = lax.all_to_all(term, "seq", split_axis=0, concat_axis=0, tiled=True)

    each = count // groups
    bases = []
    for flip in range(groups):
        sums = lax.dynamic_slice_in_dim(arrived, (group ^ flip) * each, each, 0)
        bases.append(grp_move(sums, flip) if flip else sums)

    grad_down = adapter_grad(rank_here[:, :ranks], mask, hidden_slab, weights)
    grad_up = adapter_grad(rank_here[:, ranks:], mask, grad_slab, weights)
    grad_hidden = join(bases, term, group)
    return grad_hidden, grad_down, grad_up


def solution(mesh):
    placed = (
        P("seq", "grp"),
        P("seq", "grp"),
        P("seq", "grp"),
        P(None, None, ("grp", "seq")),
        P(None, None, ("grp", "seq")),
        P(),
        P(),
    )
    return jax.shard_map(
        shards,
        mesh=mesh,
        in_specs=placed,
        out_specs=(P("seq", "grp"), P(None, None, ("grp", "seq")), P(None, None, ("grp", "seq"))),
        check_vma=False,
    )
```

```python
import functools

import jax
import jax.numpy as jnp
from jax import lax
from jax.experimental import pallas as pl
from jax.experimental.pallas import tpu as pltpu
from jax.sharding import PartitionSpec as P

ADAPTER_SCALE = 2.0
CONTRACT_LAST = (((1,), (1,)), ((), ()))
CONTRACT_ROWS = (((0,), (0,)), ((), ()))
CORES = 2
MOST_ROWS = 1024
STREAMS = 2
ANYWHERE = pl.BlockSpec(memory_space=pl.ANY)


def dot(left, right, dims):
    return lax.dot_general(left, right, dims, preferred_element_type=jnp.float32)


def pieces(total):
    step = min(total, MOST_ROWS)
    return [(at, min(step, total - at)) for at in range(0, total, step)]


def tile_of(width):
    fits = [tile for tile in (512, 448, 384, 256, 128) if width % tile == 0 and tile % 128 == 0]
    return fits[0] if fits else width


def chunk_kernel(stages, streams, place_ref, near_ref, far_ref, *rest):
    weights, outs, rows = rest[: 2 * streams], rest[-5:-1], rest[-1]
    part = near_ref.shape[0] // (2 * len(stages))
    sides = [(ref, flips) for ref, order in zip((near_ref, far_ref), stages) for flips in order]
    cuts = [(ref, flip) for ref, flips in sides for flip in flips]

    @pl.when(pl.program_id(0) == 0)
    def _():
        for at, (ref, flip) in enumerate(cuts):
            low = pl.multiple_of((place_ref[0] ^ flip) * part, part)
            rows[at * part : (at + 1) * part] = ref[pl.ds(low, part)]

    size, depth = weights[0].shape
    for stream in range(streams):
        full = sum(
            dot(rows[:, half * depth : (half + 1) * depth], weights[2 * stream + half][...], CONTRACT_LAST)
            for half in range(2)
        ).astype(jnp.bfloat16)
        for at in range(len(cuts)):
            outs[at // 2][at % 2, :, stream * size : (stream + 1) * size] = full[
                at * part : (at + 1) * part
            ]


STAGES = (((0, 2), (1, 3)), ((0, 1), (2, 3)))


def chunk_product(near, far, weight, group, *gates):
    block, depth = near.shape
    width = weight.shape[0]
    tile = tile_of(width)
    part = block // (2 * len(STAGES))
    streams = STREAMS if tile % (128 * STREAMS) == 0 else 1

    def piece(stream, half):
        return lambda at, place: (at * streams + stream, half)

    return pl.pallas_call(
        functools.partial(chunk_kernel, STAGES, streams),
        grid_spec=pltpu.PrefetchScalarGridSpec(
            num_scalar_prefetch=1,
            grid=(width // tile,),
            in_specs=[
                pl.BlockSpec((block, depth), lambda at, place: (0, 0)),
                pl.BlockSpec((block, depth), lambda at, place: (0, 0)),
            ]
            + [
                pl.BlockSpec((tile // streams, depth // 2), piece(stream, half))
                for stream in range(streams)
                for half in range(2)
            ]
            + [ANYWHERE] * len(gates),
            out_specs=[pl.BlockSpec((2, part, tile), lambda at, place: (0, 0, at))] * 4,
            scratch_shapes=[pltpu.VMEM((CORES * block, depth), jnp.bfloat16)],
        ),
        out_shape=[jax.ShapeDtypeStruct((2, part, width), jnp.bfloat16)] * 4,
        compiler_params=pltpu.CompilerParams(vmem_limit_bytes=52 << 20),
        cost_estimate=pl.CostEstimate(
            flops=2 * CORES * block * depth * width,
            bytes_accessed=2 * (width * depth + CORES * block * (depth + width)),
            transcendentals=0,
        ),
    )(group.reshape(1), near, far, *[weight] * (2 * streams), *gates)


def cut_kernel(rows_ref, out_ref):
    out_ref[0] = rows_ref[...]


def cut_columns(rows, count):
    block, width = rows.shape
    slab = width // count
    if slab % 128:
        return rows.reshape(block, count, slab).transpose(1, 0, 2)
    return pl.pallas_call(
        cut_kernel,
        grid=(count,),
        in_specs=[pl.BlockSpec((block, slab), lambda at: (0, at))],
        out_specs=pl.BlockSpec((1, block, slab), lambda at: (at, 0, 0)),
        out_shape=jax.ShapeDtypeStruct((count, block, slab), rows.dtype),
        compiler_params=pltpu.CompilerParams(vmem_limit_bytes=4 << 20),
        cost_estimate=pl.CostEstimate(flops=0, bytes_accessed=4 * rows.size, transcendentals=0),
    )(rows)


def touch_kernel(*refs):
    pass


def touch(value, *gates):
    return pl.pallas_call(
        touch_kernel,
        in_specs=[ANYWHERE] * (1 + len(gates)),
        out_specs=ANYWHERE,
        out_shape=jax.ShapeDtypeStruct(value.shape, value.dtype),
        input_output_aliases={0: 0},
        compiler_params=pltpu.CompilerParams(vmem_limit_bytes=1 << 20),
    )(value, *gates)


def join_kernel(groups, slab, place_ref, *refs):
    bases, term_ref, out_ref = refs[:groups], refs[groups], refs[groups + 1]
    width = bases[0].shape[2]
    for flip in range(groups):

        @pl.when(pl.program_id(0) == flip)
        def _():
            for at in range(term_ref.shape[0]):
                low = at * slab
                base = bases[flip][low // width, :, low % width : low % width + slab]
                total = base.astype(jnp.float32) + term_ref[at].astype(jnp.float32)
                out_ref[:, low : low + slab] = total.astype(jnp.bfloat16)


def join(bases, term, group):
    groups = len(bases)
    each, part, width = bases[0].shape
    count, block, slab = term.shape
    if slab % 128:
        base = jnp.zeros((groups, part, each, width), jnp.bfloat16)
        for flip, rows in enumerate(bases):
            base = lax.dynamic_update_index_in_dim(base, rows.transpose(1, 0, 2), group ^ flip, 0)
        total = base.reshape(block, -1).astype(jnp.float32)
        return (total + term.transpose(1, 0, 2).reshape(block, -1)).astype(jnp.bfloat16)
    return pl.pallas_call(
        functools.partial(join_kernel, groups, slab),
        grid_spec=pltpu.PrefetchScalarGridSpec(
            num_scalar_prefetch=1,
            grid=(groups,),
            in_specs=[pl.BlockSpec((each, part, width), lambda at, place: (0, 0, 0))] * groups
            + [pl.BlockSpec((count, part, slab), lambda at, place: (0, place[0] ^ at, 0))],
            out_specs=pl.BlockSpec((part, each * width), lambda at, place: (place[0] ^ at, 0)),
        ),
        out_shape=jax.ShapeDtypeStruct((block, each * width), jnp.bfloat16),
        compiler_params=pltpu.CompilerParams(vmem_limit_bytes=24 << 20),
        cost_estimate=pl.CostEstimate(
            flops=block * each * width, bytes_accessed=6 * block * each * width, transcendentals=0
        ),
    )(group.reshape(1), *bases, term)


def add(*terms):
    return sum(term.astype(jnp.float32) for term in terms).astype(jnp.bfloat16)


def after(value, *others):
    return lax.optimization_barrier((value,) + others)[0]


def project(rows, adapter, mask):
    tenants, ranks, width = adapter.shape
    flat = adapter.reshape(tenants * ranks, width)
    parts = []
    for at, size in pieces(rows.shape[0]):
        full = dot(rows[at : at + size], flat, CONTRACT_LAST)
        chosen = full.reshape(size, tenants, ranks) * mask[at : at + size, :, None]
        parts.append(jnp.sum(chosen, axis=1))
    return jnp.concatenate(parts, axis=0).astype(jnp.bfloat16)


def spread(rank, mask):
    wide = rank[:, None, :] * mask.astype(jnp.bfloat16)[:, :, None]
    return wide.reshape(rank.shape[0], -1)


def adapter_grad(rank, mask, rows, weights):
    tenants, ranks = mask.shape[1], rank.shape[1]
    parts = []
    for at, size in pieces(tenants * ranks):
        low, high = at // ranks, (at + size) // ranks
        grad = dot(spread(rank, mask[:, low:high]), rows, CONTRACT_ROWS)
        parts.append(grad.reshape(high - low, ranks, -1) * weights[low:high, None, None])
    return jnp.concatenate(parts, axis=0)


def shards(grad_output, hidden, down_weight, adapter_down, adapter_up, job_tenant, job_count):
    index = lax.axis_index("seq")
    group = lax.axis_index("grp")
    count = lax.axis_size("seq")
    groups = lax.axis_size("grp")
    chips = count // CORES
    chip, core = index // CORES, index % CORES
    block = grad_output.shape[0]
    tenants, ranks, down_slab = adapter_down.shape
    up_slab = adapter_up.shape[2]
    width = down_weight.shape[0]
    part = block // groups

    named = (job_tenant[:, :, None] == jnp.arange(tenants, dtype=jnp.int32)).astype(jnp.float32)
    totals = jnp.sum(job_count.astype(jnp.float32)[:, :, None] * named, axis=(0, 1))
    weights = ADAPTER_SCALE / totals
    ends = jnp.cumsum(job_count, axis=1)
    places = jnp.arange(block, dtype=jnp.int32)[None, :, None]
    member = (places >= (ends - job_count)[:, None, :]) & (places < ends[:, None, :])
    owner = jnp.sum(jnp.where(member, job_tenant[:, None, :], 0), axis=2).reshape(count * block)
    mask = (owner[:, None] == jnp.arange(tenants, dtype=jnp.int32)).astype(jnp.float32)

    def seq_move(value, chips_back, flip):
        pairs = [
            (s, ((s // CORES - chips_back) % chips) * CORES + ((s % CORES) ^ flip))
            for s in range(count)
        ]
        return lax.ppermute(value, "seq", pairs)

    def grp_move(value, flip):
        return lax.ppermute(value, "grp", [(g, g ^ flip) for g in range(groups)])

    last = chips - 1
    held, pairs, products = [grad_output], [], []
    for step in range(chips):
        if step:
            came = seq_move(held[-1], -1, 0)
            held.append(touch(came, products[step - 2][0]) if step > 1 else came)
        pairs.append((held[step], seq_move(held[step], 0, 1)))
        if step < last:
            products.append(chunk_product(*pairs[step], down_weight, group))

    cut = touch(cut_columns(hidden, count), held[1])
    hidden_slab = lax.all_to_all(cut, "seq", split_axis=0, concat_axis=0, tiled=True)
    hidden_slab = touch(hidden_slab.reshape(count * block, down_slab), products[last - 1][0])

    grad_slab = jnp.zeros((count, block, up_slab), jnp.bfloat16)
    for step, pair in enumerate(pairs):
        back = ((chip - step) % chips) * CORES
        for flip, rows in enumerate(pair):
            columns = lax.dynamic_slice_in_dim(rows, index * up_slab, up_slab, 1)
            grad_slab = lax.dynamic_update_index_in_dim(grad_slab, columns, back + (core ^ flip), 0)
    grad_slab = grad_slab.reshape(count * block, up_slab)
    ranked = jnp.concatenate(
        [project(grad_slab, adapter_up, mask), project(hidden_slab, adapter_down, mask)], axis=1
    )
    products.append(chunk_product(*pairs[last], down_weight, group, ranked))

    firsts = [
        (grp_move(near_sent, 1), grp_move(far_sent, 2)) for _, near_sent, _, far_sent in products
    ]

    def second(step, *gates):
        near_kept, _, far_kept, _ = products[step]
        near_came, far_came = firsts[step]
        near_came, far_came = lax.optimization_barrier((near_came, far_came) + gates)[:2]
        near_sum = add(near_kept[1], near_came[1])
        far_sum = add(far_kept[1], far_came[1])
        return near_sum, (grp_move(near_sum, 2), grp_move(far_sum, 1))

    def total(step, seconds, *gates):
        near_kept, _, far_kept, _ = products[step]
        near_came, far_came = firsts[step]
        near_last, far_last = lax.optimization_barrier(seconds + gates)[:2]
        return (
            add(near_kept[0], near_came[0], near_last),
            add(far_kept[0], far_came[0], far_last),
        )

    arrived = jnp.zeros((count, part, width), jnp.bfloat16)

    def hop(step, sums):
        return [
            sums[flip] if step == 0 and flip == 0 else seq_move(sums[flip], step, flip)
            for flip in range(CORES)
        ]

    def put(arrived, step, came, *gates):
        ahead = ((chip + step) % chips) * CORES
        came = lax.optimization_barrier(tuple(came) + gates)
        for flip in range(CORES):
            arrived = lax.dynamic_update_index_in_dim(arrived, came[flip], ahead + (core ^ flip), 0)
        return arrived

    came = None
    for step in range(last - 1):
        _, seconds = second(step, products[step + 1][0])
        sums = total(step, seconds)
        if came is not None:
            arrived = put(arrived, step - 1, came, sums[0])
        came = hop(step, sums)

    begun, seconds = second(last - 1, products[last][0])
    devices = count * groups
    share = lax.all_to_all(
        ranked.reshape(devices, -1, 2 * ranks),
        ("grp", "seq"),
        split_axis=0,
        concat_axis=0,
        tiled=True,
    )
    sums = total(last - 1, seconds, ranked)
    arrived = put(arrived, last - 2, came, sums[0])
    came = hop(last - 1, sums)
    begun, seconds = second(last, sums[0])
    share = after(share, begun)
    share = jnp.sum(share.astype(jnp.float32), axis=0).astype(jnp.bfloat16)
    ranked = lax.all_to_all(
        jnp.broadcast_to(share[None], (devices,) + share.shape),
        ("grp", "seq"),
        split_axis=0,
        concat_axis=0,
        tiled=True,
    ).reshape(count * block, 2 * ranks)
    sums = total(last, seconds, share)
    arrived = put(arrived, last - 1, came, sums[0])
    came = hop(last, sums)
    ranked = after(ranked, *sums)
    grad_rank = ranked[:, :ranks]

    flat_down = adapter_down.reshape(tenants * ranks, down_slab)
    term = jnp.concatenate(
        [
            jnp.dot(
                spread(grad_rank[at : at + size], mask[at : at + size]),
                flat_down,
                preferred_element_type=jnp.float32,
            )
            for at, size in pieces(count * block)
        ],
        axis=0,
    )
    term = (term * ADAPTER_SCALE).astype(jnp.bfloat16).reshape(count, block, down_slab)
    arrived = put(arrived, last, came, term)
    rank_here = after(ranked, term)
    term = lax.all_to_all(term, "seq", split_axis=0, concat_axis=0, tiled=True)

    each = count // groups
    bases = []
    for flip in range(groups):
        sums = lax.dynamic_slice_in_dim(arrived, (group ^ flip) * each, each, 0)
        bases.append(grp_move(sums, flip) if flip else sums)

    grad_down = adapter_grad(rank_here[:, :ranks], mask, hidden_slab, weights)
    grad_up = adapter_grad(rank_here[:, ranks:], mask, grad_slab, weights)
    grad_hidden = join(bases, term, group)
    return grad_hidden, grad_down, grad_up


def solution(mesh):
    placed = (
        P("seq", "grp"),
        P("seq", "grp"),
        P("seq", "grp"),
        P(None, None, ("grp", "seq")),
        P(None, None, ("grp", "seq")),
        P(),
        P(),
    )
    return jax.shard_map(
        shards,
        mesh=mesh,
        in_specs=placed,
        out_specs=(P("seq", "grp"), P(None, None, ("grp", "seq")), P(None, None, ("grp", "seq"))),
        check_vma=False,
    )
```

```python
import functools

import jax
import jax.numpy as jnp
from jax import lax
from jax.experimental import pallas as pl
from jax.experimental.pallas import tpu as pltpu
from jax.sharding import PartitionSpec as P

ADAPTER_SCALE = 2.0
CONTRACT_LAST = (((1,), (1,)), ((), ()))
CONTRACT_ROWS = (((0,), (0,)), ((), ()))
CORES = 2
MOST_ROWS = 1024
ANYWHERE = pl.BlockSpec(memory_space=pl.ANY)


def dot(left, right, dims):
    return lax.dot_general(left, right, dims, preferred_element_type=jnp.float32)


def pieces(total):
    step = min(total, MOST_ROWS)
    return [(at, min(step, total - at)) for at in range(0, total, step)]


def tile_of(width):
    fits = [tile for tile in (512, 448, 384, 256, 128) if width % tile == 0 and tile % 128 == 0]
    return fits[0] if fits else width


def chunk_kernel(stages, place_ref, near_ref, far_ref, weight_ref, *rest):
    outs, rows = rest[-5:-1], rest[-1]
    part = near_ref.shape[0] // (2 * len(stages))
    sides = [(ref, flips) for ref, order in zip((near_ref, far_ref), stages) for flips in order]
    cuts = [(ref, flip) for ref, flips in sides for flip in flips]

    @pl.when(pl.program_id(0) == 0)
    def _():
        for at, (ref, flip) in enumerate(cuts):
            low = pl.multiple_of((place_ref[0] ^ flip) * part, part)
            rows[at * part : (at + 1) * part] = ref[pl.ds(low, part)]

    full = dot(rows[...], weight_ref[...], CONTRACT_LAST).astype(jnp.bfloat16)
    for at in range(len(cuts)):
        outs[at // 2][at % 2] = full[at * part : (at + 1) * part]


STAGES = (((0, 2), (1, 3)), ((0, 1), (2, 3)))


def chunk_product(near, far, weight, group, *gates):
    block, depth = near.shape
    width = weight.shape[0]
    tile = tile_of(width)
    part = block // (2 * len(STAGES))
    return pl.pallas_call(
        functools.partial(chunk_kernel, STAGES),
        grid_spec=pltpu.PrefetchScalarGridSpec(
            num_scalar_prefetch=1,
            grid=(width // tile,),
            in_specs=[
                pl.BlockSpec((block, depth), lambda at, place: (0, 0)),
                pl.BlockSpec((block, depth), lambda at, place: (0, 0)),
                pl.BlockSpec((tile, depth), lambda at, place: (at, 0)),
            ]
            + [ANYWHERE] * len(gates),
            out_specs=[pl.BlockSpec((2, part, tile), lambda at, place: (0, 0, at))] * 4,
            scratch_shapes=[pltpu.VMEM((CORES * block, depth), jnp.bfloat16)],
        ),
        out_shape=[jax.ShapeDtypeStruct((2, part, width), jnp.bfloat16)] * 4,
        compiler_params=pltpu.CompilerParams(vmem_limit_bytes=24 << 20),
        cost_estimate=pl.CostEstimate(
            flops=2 * CORES * block * depth * width,
            bytes_accessed=2 * (width * depth + CORES * block * (depth + width)),
            transcendentals=0,
        ),
    )(group.reshape(1), near, far, weight, *gates)


def join_kernel(groups, slab, place_ref, *refs):
    bases, term_ref, out_ref = refs[:groups], refs[groups], refs[groups + 1]
    width = bases[0].shape[2]
    for flip in range(groups):

        @pl.when(pl.program_id(0) == flip)
        def _():
            for at in range(term_ref.shape[0]):
                low = at * slab
                base = bases[flip][low // width, :, low % width : low % width + slab]
                total = base.astype(jnp.float32) + term_ref[at].astype(jnp.float32)
                out_ref[:, low : low + slab] = total.astype(jnp.bfloat16)


def join(bases, term, group):
    groups = len(bases)
    each, part, width = bases[0].shape
    count, block, slab = term.shape
    if slab % 128:
        base = jnp.zeros((groups, part, each, width), jnp.bfloat16)
        for flip, rows in enumerate(bases):
            base = lax.dynamic_update_index_in_dim(base, rows.transpose(1, 0, 2), group ^ flip, 0)
        total = base.reshape(block, -1).astype(jnp.float32)
        return (total + term.transpose(1, 0, 2).reshape(block, -1)).astype(jnp.bfloat16)
    return pl.pallas_call(
        functools.partial(join_kernel, groups, slab),
        grid_spec=pltpu.PrefetchScalarGridSpec(
            num_scalar_prefetch=1,
            grid=(groups,),
            in_specs=[pl.BlockSpec((each, part, width), lambda at, place: (0, 0, 0))] * groups
            + [pl.BlockSpec((count, part, slab), lambda at, place: (0, place[0] ^ at, 0))],
            out_specs=pl.BlockSpec((part, each * width), lambda at, place: (place[0] ^ at, 0)),
        ),
        out_shape=jax.ShapeDtypeStruct((block, each * width), jnp.bfloat16),
        compiler_params=pltpu.CompilerParams(vmem_limit_bytes=24 << 20),
        cost_estimate=pl.CostEstimate(
            flops=block * each * width, bytes_accessed=6 * block * each * width, transcendentals=0
        ),
    )(group.reshape(1), *bases, term)


def add(*terms):
    return sum(term.astype(jnp.float32) for term in terms).astype(jnp.bfloat16)


def touch_kernel(*refs):
    pass


def touch(values, *gates):
    return pl.pallas_call(
        touch_kernel,
        in_specs=[ANYWHERE] * (len(values) + len(gates)),
        out_specs=[ANYWHERE] * len(values),
        out_shape=[jax.ShapeDtypeStruct(value.shape, value.dtype) for value in values],
        input_output_aliases={at: at for at in range(len(values))},
        compiler_params=pltpu.CompilerParams(vmem_limit_bytes=1 << 20),
    )(*values, *gates)


def after(value, *others):
    return lax.optimization_barrier((value,) + others)[0]


def project(rows, adapter, mask):
    tenants, ranks, width = adapter.shape
    flat = adapter.reshape(tenants * ranks, width)
    parts = []
    for at, size in pieces(rows.shape[0]):
        full = dot(rows[at : at + size], flat, CONTRACT_LAST)
        chosen = full.reshape(size, tenants, ranks) * mask[at : at + size, :, None]
        parts.append(jnp.sum(chosen, axis=1))
    return jnp.concatenate(parts, axis=0).astype(jnp.bfloat16)


def spread(rank, mask):
    wide = rank[:, None, :] * mask.astype(jnp.bfloat16)[:, :, None]
    return wide.reshape(rank.shape[0], -1)


def adapter_grad(rank, mask, rows, weights):
    tenants, ranks = mask.shape[1], rank.shape[1]
    parts = []
    for at, size in pieces(tenants * ranks):
        low, high = at // ranks, (at + size) // ranks
        grad = dot(spread(rank, mask[:, low:high]), rows, CONTRACT_ROWS)
        parts.append(grad.reshape(high - low, ranks, -1) * weights[low:high, None, None])
    return jnp.concatenate(parts, axis=0)


def shards(grad_output, hidden, down_weight, adapter_down, adapter_up, job_tenant, job_count):
    index = lax.axis_index("seq")
    group = lax.axis_index("grp")
    count = lax.axis_size("seq")
    groups = lax.axis_size("grp")
    chips = count // CORES
    chip, core = index // CORES, index % CORES
    block = grad_output.shape[0]
    tenants, ranks, down_slab = adapter_down.shape
    up_slab = adapter_up.shape[2]
    width = down_weight.shape[0]
    part = block // groups

    named = (job_tenant[:, :, None] == jnp.arange(tenants, dtype=jnp.int32)).astype(jnp.float32)
    totals = jnp.sum(job_count.astype(jnp.float32)[:, :, None] * named, axis=(0, 1))
    weights = ADAPTER_SCALE / totals
    ends = jnp.cumsum(job_count, axis=1)
    places = jnp.arange(block, dtype=jnp.int32)[None, :, None]
    member = (places >= (ends - job_count)[:, None, :]) & (places < ends[:, None, :])
    owner = jnp.sum(jnp.where(member, job_tenant[:, None, :], 0), axis=2).reshape(count * block)
    mask = (owner[:, None] == jnp.arange(tenants, dtype=jnp.int32)).astype(jnp.float32)

    def seq_move(value, chips_back, flip):
        pairs = [
            (s, ((s // CORES - chips_back) % chips) * CORES + ((s % CORES) ^ flip))
            for s in range(count)
        ]
        return lax.ppermute(value, "seq", pairs)

    def grp_move(value, flip):
        return lax.ppermute(value, "grp", [(g, g ^ flip) for g in range(groups)])

    held = [grad_output]
    for step in range(1, chips):
        held.append(seq_move(held[-1], -1, 0))
    pairs = [(near, seq_move(near, 0, 1)) for near in held]

    hidden_slab = lax.all_to_all(
        hidden.reshape(block, count, down_slab).transpose(1, 0, 2),
        "seq",
        split_axis=0,
        concat_axis=0,
        tiled=True,
    ).reshape(count * block, down_slab)

    last = chips - 1
    grad_slab = jnp.zeros((count, block, up_slab), jnp.bfloat16)
    for step, pair in enumerate(pairs):
        back = ((chip - step) % chips) * CORES
        for flip, rows in enumerate(pair):
            columns = lax.dynamic_slice_in_dim(rows, index * up_slab, up_slab, 1)
            grad_slab = lax.dynamic_update_index_in_dim(grad_slab, columns, back + (core ^ flip), 0)
    grad_slab = grad_slab.reshape(count * block, up_slab)
    ranked = jnp.concatenate(
        [project(grad_slab, adapter_up, mask), project(hidden_slab, adapter_down, mask)], axis=1
    )

    products = [
        chunk_product(near, far, down_weight, group, *([ranked] if step == last else []))
        for step, (near, far) in enumerate(pairs)
    ]
    firsts = [
        (grp_move(near_sent, 1), grp_move(far_sent, 2)) for _, near_sent, _, far_sent in products
    ]

    def second(step, *gates):
        near_kept, _, far_kept, _ = products[step]
        near_came, far_came = firsts[step]
        near_came, far_came = lax.optimization_barrier((near_came, far_came) + gates)[:2]
        near_sum = add(near_kept[1], near_came[1])
        far_sum = add(far_kept[1], far_came[1])
        return near_sum, (grp_move(near_sum, 2), grp_move(far_sum, 1))

    def total(step, seconds, *gates):
        near_kept, _, far_kept, _ = products[step]
        near_came, far_came = firsts[step]
        near_last, far_last = lax.optimization_barrier(seconds + gates)[:2]
        return (
            add(near_kept[0], near_came[0], near_last),
            add(far_kept[0], far_came[0], far_last),
        )

    arrived = jnp.zeros((count, part, width), jnp.bfloat16)

    def hop(step, sums):
        return [
            sums[flip] if step == 0 and flip == 0 else seq_move(sums[flip], step, flip)
            for flip in range(CORES)
        ]

    def put(arrived, step, came, *gates):
        ahead = ((chip + step) % chips) * CORES
        came = lax.optimization_barrier(tuple(came) + gates)
        for flip in range(CORES):
            arrived = lax.dynamic_update_index_in_dim(arrived, came[flip], ahead + (core ^ flip), 0)
        return arrived

    came = None
    for step in range(last - 1):
        _, seconds = second(step, products[step + 1][0])
        sums = total(step, seconds)
        if came is not None:
            arrived = put(arrived, step - 1, came, sums[0])
        came = hop(step, sums)

    devices = count * groups
    share = lax.all_to_all(
        ranked.reshape(devices, -1, 2 * ranks),
        ("grp", "seq"),
        split_axis=0,
        concat_axis=0,
        tiled=True,
    )
    firsts[last - 1] = touch(firsts[last - 1], share)
    _, seconds = second(last - 1, products[last][0])
    sums = total(last - 1, seconds)
    arrived = put(arrived, last - 2, came, sums[0])
    came = hop(last - 1, sums)
    _, seconds = second(last, sums[0])
    share = jnp.sum(share.astype(jnp.float32), axis=0).astype(jnp.bfloat16)
    ranked = lax.all_to_all(
        jnp.broadcast_to(share[None], (devices,) + share.shape),
        ("grp", "seq"),
        split_axis=0,
        concat_axis=0,
        tiled=True,
    ).reshape(count * block, 2 * ranks)
    sums = total(last, seconds, share)
    arrived = put(arrived, last - 1, came, sums[0])
    came = hop(last, sums)
    ranked = after(ranked, *sums)
    grad_rank = ranked[:, :ranks]

    flat_down = adapter_down.reshape(tenants * ranks, down_slab)
    term = jnp.concatenate(
        [
            jnp.dot(
                spread(grad_rank[at : at + size], mask[at : at + size]),
                flat_down,
                preferred_element_type=jnp.float32,
            )
            for at, size in pieces(count * block)
        ],
        axis=0,
    )
    term = (term * ADAPTER_SCALE).astype(jnp.bfloat16).reshape(count, block, down_slab)
    arrived = put(arrived, last, came, term)
    rank_here = after(ranked, term)
    term = lax.all_to_all(term, "seq", split_axis=0, concat_axis=0, tiled=True)

    each = count // groups
    bases = []
    for flip in range(groups):
        sums = lax.dynamic_slice_in_dim(arrived, (group ^ flip) * each, each, 0)
        bases.append(grp_move(sums, flip) if flip else sums)

    grad_down = adapter_grad(rank_here[:, :ranks], mask, hidden_slab, weights)
    grad_up = adapter_grad(rank_here[:, ranks:], mask, grad_slab, weights)
    grad_hidden = join(bases, term, group)
    return grad_hidden, grad_down, grad_up


def solution(mesh):
    placed = (
        P("seq", "grp"),
        P("seq", "grp"),
        P("seq", "grp"),
        P(None, None, ("grp", "seq")),
        P(None, None, ("grp", "seq")),
        P(),
        P(),
    )
    return jax.shard_map(
        shards,
        mesh=mesh,
        in_specs=placed,
        out_specs=(P("seq", "grp"), P(None, None, ("grp", "seq")), P(None, None, ("grp", "seq"))),
        check_vma=False,
    )
```

```python
import functools

import jax
import jax.numpy as jnp
from jax import lax
from jax.experimental import pallas as pl
from jax.experimental.pallas import tpu as pltpu
from jax.sharding import PartitionSpec as P

ADAPTER_SCALE = 2.0
CONTRACT_LAST = (((1,), (1,)), ((), ()))
CONTRACT_ROWS = (((0,), (0,)), ((), ()))
CORES = 2
MOST_ROWS = 1024
ANYWHERE = pl.BlockSpec(memory_space=pl.ANY)


def dot(left, right, dims):
    return lax.dot_general(left, right, dims, preferred_element_type=jnp.float32)


def pieces(total):
    step = min(total, MOST_ROWS)
    return [(at, min(step, total - at)) for at in range(0, total, step)]


def tile_of(width):
    fits = [tile for tile in (512, 448, 384, 256, 128) if width % tile == 0 and tile % 128 == 0]
    return fits[0] if fits else width


def chunk_kernel(groups, place_ref, near_ref, far_ref, weight_ref, *rest):
    outs, rows = rest[-groups - 1 : -1], rest[-1]
    part = near_ref.shape[0] // groups

    @pl.when(pl.program_id(0) == 0)
    def _():
        for flip in range(groups):
            at = pl.multiple_of((place_ref[0] ^ flip) * part, part)
            low = flip * CORES * part
            rows[low : low + part] = near_ref[pl.ds(at, part)]
            rows[low + part : low + 2 * part] = far_ref[pl.ds(at, part)]

    full = dot(rows[...], weight_ref[...], CONTRACT_LAST).astype(jnp.bfloat16)
    for flip in range(groups):
        for core in range(CORES):
            low = (flip * CORES + core) * part
            outs[flip][core] = full[low : low + part]


def chunk_product(near, far, weight, group, groups, *gates):
    block, depth = near.shape
    width = weight.shape[0]
    tile = tile_of(width)
    part = block // groups
    return pl.pallas_call(
        functools.partial(chunk_kernel, groups),
        grid_spec=pltpu.PrefetchScalarGridSpec(
            num_scalar_prefetch=1,
            grid=(width // tile,),
            in_specs=[
                pl.BlockSpec((block, depth), lambda at, place: (0, 0)),
                pl.BlockSpec((block, depth), lambda at, place: (0, 0)),
                pl.BlockSpec((tile, depth), lambda at, place: (at, 0)),
            ]
            + [ANYWHERE] * len(gates),
            out_specs=[pl.BlockSpec((CORES, part, tile), lambda at, place: (0, 0, at))] * groups,
            scratch_shapes=[pltpu.VMEM((CORES * block, depth), jnp.bfloat16)],
        ),
        out_shape=[jax.ShapeDtypeStruct((CORES, part, width), jnp.bfloat16)] * groups,
        compiler_params=pltpu.CompilerParams(vmem_limit_bytes=24 << 20),
        cost_estimate=pl.CostEstimate(
            flops=2 * CORES * block * depth * width,
            bytes_accessed=2 * (width * depth + CORES * block * (depth + width)),
            transcendentals=0,
        ),
    )(group.reshape(1), near, far, weight, *gates)


def join_kernel(groups, slab, place_ref, *refs):
    bases, term_ref, out_ref = refs[:groups], refs[groups], refs[groups + 1]
    width = bases[0].shape[2]
    for flip in range(groups):

        @pl.when(pl.program_id(0) == flip)
        def _():
            for at in range(term_ref.shape[0]):
                low = at * slab
                base = bases[flip][low // width, :, low % width : low % width + slab]
                total = base.astype(jnp.float32) + term_ref[at].astype(jnp.float32)
                out_ref[:, low : low + slab] = total.astype(jnp.bfloat16)


def join(bases, term, group):
    groups = len(bases)
    each, part, width = bases[0].shape
    count, block, slab = term.shape
    if slab % 128:
        base = jnp.zeros((groups, part, each, width), jnp.bfloat16)
        for flip, rows in enumerate(bases):
            base = lax.dynamic_update_index_in_dim(base, rows.transpose(1, 0, 2), group ^ flip, 0)
        total = base.reshape(block, -1).astype(jnp.float32)
        return (total + term.transpose(1, 0, 2).reshape(block, -1)).astype(jnp.bfloat16)
    return pl.pallas_call(
        functools.partial(join_kernel, groups, slab),
        grid_spec=pltpu.PrefetchScalarGridSpec(
            num_scalar_prefetch=1,
            grid=(groups,),
            in_specs=[pl.BlockSpec((each, part, width), lambda at, place: (0, 0, 0))] * groups
            + [pl.BlockSpec((count, part, slab), lambda at, place: (0, place[0] ^ at, 0))],
            out_specs=pl.BlockSpec((part, each * width), lambda at, place: (place[0] ^ at, 0)),
        ),
        out_shape=jax.ShapeDtypeStruct((block, each * width), jnp.bfloat16),
        compiler_params=pltpu.CompilerParams(vmem_limit_bytes=24 << 20),
        cost_estimate=pl.CostEstimate(
            flops=block * each * width, bytes_accessed=6 * block * each * width, transcendentals=0
        ),
    )(group.reshape(1), *bases, term)


def add(*terms):
    return sum(term.astype(jnp.float32) for term in terms).astype(jnp.bfloat16)


def touch_kernel(*refs):
    pass


def touch(values, *gates):
    return pl.pallas_call(
        touch_kernel,
        in_specs=[ANYWHERE] * (len(values) + len(gates)),
        out_specs=[ANYWHERE] * len(values),
        out_shape=[jax.ShapeDtypeStruct(value.shape, value.dtype) for value in values],
        input_output_aliases={at: at for at in range(len(values))},
        compiler_params=pltpu.CompilerParams(vmem_limit_bytes=1 << 20),
    )(*values, *gates)


def after(value, *others):
    return lax.optimization_barrier((value,) + others)[0]


def project(rows, adapter, mask):
    tenants, ranks, width = adapter.shape
    flat = adapter.reshape(tenants * ranks, width)
    parts = []
    for at, size in pieces(rows.shape[0]):
        full = dot(rows[at : at + size], flat, CONTRACT_LAST)
        chosen = full.reshape(size, tenants, ranks) * mask[at : at + size, :, None]
        parts.append(jnp.sum(chosen, axis=1))
    return jnp.concatenate(parts, axis=0).astype(jnp.bfloat16)


def project_kernel(owner_ref, grad_ref, act_ref, up_ref, down_ref, out_ref):
    rows, lanes = out_ref.shape
    owner = owner_ref[...]
    lane = lax.broadcasted_iota(jnp.int32, (rows, lanes), 1)
    high = (lane >= lanes // 2).astype(jnp.int32)

    def pick(left, adapter):
        full = dot(left, adapter, CONTRACT_LAST)
        total = jnp.zeros((rows, lanes), jnp.float32)
        for pair in range(full.shape[1] // lanes):
            mine = owner == 2 * pair + high
            total += jnp.where(mine, full[:, pair * lanes : (pair + 1) * lanes], 0.0)
        return total + pltpu.roll(total, lanes // 2, 1)

    grad = pick(grad_ref[...], up_ref[...])
    act = pick(act_ref[...], down_ref[...])
    out_ref[...] = jnp.where(high == 0, grad, act).astype(jnp.bfloat16)


def project_both(grad_slab, hidden_slab, adapter_up, adapter_down, owner, mask):
    tenants, ranks, up_slab = adapter_up.shape
    down_slab = adapter_down.shape[2]
    tokens = grad_slab.shape[0]
    rows = 256
    if up_slab % 128 or down_slab % 128 or ranks != 64 or tenants % 2 or tokens % rows:
        return jnp.concatenate(
            [project(grad_slab, adapter_up, mask), project(hidden_slab, adapter_down, mask)], axis=1
        )
    return pl.pallas_call(
        project_kernel,
        grid=(tokens // rows,),
        in_specs=[
            pl.BlockSpec((rows, 1), lambda at: (at, 0)),
            pl.BlockSpec((rows, up_slab), lambda at: (at, 0)),
            pl.BlockSpec((rows, down_slab), lambda at: (at, 0)),
            pl.BlockSpec((tenants * ranks, up_slab), lambda at: (0, 0)),
            pl.BlockSpec((tenants * ranks, down_slab), lambda at: (0, 0)),
        ],
        out_specs=pl.BlockSpec((rows, 2 * ranks), lambda at: (at, 0)),
        out_shape=jax.ShapeDtypeStruct((tokens, 2 * ranks), jnp.bfloat16),
        compiler_params=pltpu.CompilerParams(vmem_limit_bytes=24 << 20),
        cost_estimate=pl.CostEstimate(
            flops=2 * tokens * tenants * ranks * (up_slab + down_slab),
            bytes_accessed=2 * (tokens + tenants * ranks) * (up_slab + down_slab),
            transcendentals=0,
        ),
    )(
        owner.reshape(tokens, 1),
        grad_slab,
        hidden_slab,
        adapter_up.reshape(tenants * ranks, up_slab),
        adapter_down.reshape(tenants * ranks, down_slab),
    )


def spread(rank, mask):
    wide = rank[:, None, :] * mask.astype(jnp.bfloat16)[:, :, None]
    return wide.reshape(rank.shape[0], -1)


def adapter_grad(rank, mask, rows, weights):
    tenants, ranks = mask.shape[1], rank.shape[1]
    parts = []
    for at, size in pieces(tenants * ranks):
        low, high = at // ranks, (at + size) // ranks
        grad = dot(spread(rank, mask[:, low:high]), rows, CONTRACT_ROWS)
        parts.append(grad.reshape(high - low, ranks, -1) * weights[low:high, None, None])
    return jnp.concatenate(parts, axis=0)


def shards(grad_output, hidden, down_weight, adapter_down, adapter_up, job_tenant, job_count):
    index = lax.axis_index("seq")
    group = lax.axis_index("grp")
    count = lax.axis_size("seq")
    groups = lax.axis_size("grp")
    chips = count // CORES
    chip, core = index // CORES, index % CORES
    block = grad_output.shape[0]
    tenants, ranks, down_slab = adapter_down.shape
    up_slab = adapter_up.shape[2]
    width = down_weight.shape[0]
    part = block // groups

    named = (job_tenant[:, :, None] == jnp.arange(tenants, dtype=jnp.int32)).astype(jnp.float32)
    totals = jnp.sum(job_count.astype(jnp.float32)[:, :, None] * named, axis=(0, 1))
    weights = ADAPTER_SCALE / totals
    ends = jnp.cumsum(job_count, axis=1)
    places = jnp.arange(block, dtype=jnp.int32)[None, :, None]
    member = (places >= (ends - job_count)[:, None, :]) & (places < ends[:, None, :])
    owner = jnp.sum(jnp.where(member, job_tenant[:, None, :], 0), axis=2).reshape(count * block)
    mask = (owner[:, None] == jnp.arange(tenants, dtype=jnp.int32)).astype(jnp.float32)

    def seq_move(value, chips_back, flip):
        pairs = [
            (s, ((s // CORES - chips_back) % chips) * CORES + ((s % CORES) ^ flip))
            for s in range(count)
        ]
        return lax.ppermute(value, "seq", pairs)

    def grp_move(value, flip):
        return lax.ppermute(value, "grp", [(g, g ^ flip) for g in range(groups)])

    held = [grad_output]
    for step in range(1, chips):
        held.append(seq_move(held[-1], -1, 0))
    pairs = [(near, seq_move(near, 0, 1)) for near in held]

    hidden_slab = lax.all_to_all(
        hidden.reshape(block, count, down_slab).transpose(1, 0, 2),
        "seq",
        split_axis=0,
        concat_axis=0,
        tiled=True,
    ).reshape(count * block, down_slab)

    last = chips - 1
    grad_slab = jnp.zeros((count, block, up_slab), jnp.bfloat16)
    for step, pair in enumerate(pairs):
        back = ((chip - step) % chips) * CORES
        for flip, rows in enumerate(pair):
            columns = lax.dynamic_slice_in_dim(rows, index * up_slab, up_slab, 1)
            grad_slab = lax.dynamic_update_index_in_dim(grad_slab, columns, back + (core ^ flip), 0)
    grad_slab = grad_slab.reshape(count * block, up_slab)
    ranked = project_both(grad_slab, hidden_slab, adapter_up, adapter_down, owner, mask)

    products = [
        chunk_product(near, far, down_weight, group, groups) for near, far in pairs
    ]
    came = []
    for step in range(chips):
        kept = products[step][0]
        others = [grp_move(products[step][flip], flip) for flip in range(1, groups)]
        gates = [products[step + 1][0]] if step < last else []
        if step == last - 1:
            gates.append(ranked)
        if gates:
            (others[0],) = touch([others[0]], *gates)
        sums = add(kept, *others)
        came.append(seq_move(sums, step, 0) if step else sums)

    devices = count * groups
    share = lax.all_to_all(
        ranked.reshape(devices, -1, 2 * ranks),
        ("grp", "seq"),
        split_axis=0,
        concat_axis=0,
        tiled=True,
    )
    share = jnp.sum(share.astype(jnp.float32), axis=0).astype(jnp.bfloat16)
    ranked = lax.all_to_all(
        jnp.broadcast_to(share[None], (devices,) + share.shape),
        ("grp", "seq"),
        split_axis=0,
        concat_axis=0,
        tiled=True,
    ).reshape(count * block, 2 * ranks)
    (ranked,) = touch([ranked], sums)
    grad_rank = ranked[:, :ranks]

    flat_down = adapter_down.reshape(tenants * ranks, down_slab)
    term = jnp.concatenate(
        [
            jnp.dot(
                spread(grad_rank[at : at + size], mask[at : at + size]),
                flat_down,
                preferred_element_type=jnp.float32,
            )
            for at, size in pieces(count * block)
        ],
        axis=0,
    )
    term = (term * ADAPTER_SCALE).astype(jnp.bfloat16).reshape(count, block, down_slab)
    rank_here = after(ranked, term)
    term = lax.all_to_all(term, "seq", split_axis=0, concat_axis=0, tiled=True)

    mine = jnp.stack([sums[0] for sums in came])
    theirs = seq_move(jnp.stack([sums[1] for sums in came]), 0, 1)
    halves = jnp.stack([mine, theirs], axis=1).reshape(count, part, width)

    each = count // groups
    bases = []
    for flip in range(groups):
        wanted = []
        for at in range(each):
            owner_at = (group ^ flip) * each + at
            ahead = (owner_at // CORES - chip) % chips
            wanted.append(
                lax.dynamic_slice_in_dim(halves, ahead * CORES + (owner_at % CORES ^ core), 1, 0)
            )
        sums = jnp.concatenate(wanted, axis=0)
        bases.append(grp_move(sums, flip) if flip else sums)

    grad_down = adapter_grad(rank_here[:, :ranks], mask, hidden_slab, weights)
    grad_up = adapter_grad(rank_here[:, ranks:], mask, grad_slab, weights)
    grad_hidden = join(bases, term, group)
    return grad_hidden, grad_down, grad_up


def solution(mesh):
    placed = (
        P("seq", "grp"),
        P("seq", "grp"),
        P("seq", "grp"),
        P(None, None, ("grp", "seq")),
        P(None, None, ("grp", "seq")),
        P(),
        P(),
    )
    return jax.shard_map(
        shards,
        mesh=mesh,
        in_specs=placed,
        out_specs=(P("seq", "grp"), P(None, None, ("grp", "seq")), P(None, None, ("grp", "seq"))),
        check_vma=False,
    )
```

```python
import functools

import jax
import jax.numpy as jnp
from jax import lax
from jax.experimental import pallas as pl
from jax.experimental.pallas import tpu as pltpu
from jax.sharding import PartitionSpec as P

ADAPTER_SCALE = 2.0
CONTRACT_LAST = (((1,), (1,)), ((), ()))
CONTRACT_ROWS = (((0,), (0,)), ((), ()))
CORES = 2
MOST_ROWS = 1024
ANYWHERE = pl.BlockSpec(memory_space=pl.ANY)


def dot(left, right, dims):
    return lax.dot_general(left, right, dims, preferred_element_type=jnp.float32)


def pieces(total):
    step = min(total, MOST_ROWS)
    return [(at, min(step, total - at)) for at in range(0, total, step)]


def tile_of(width):
    fits = [tile for tile in (512, 448, 384, 256, 128) if width % tile == 0 and tile % 128 == 0]
    return fits[0] if fits else width


def chunk_kernel(groups, place_ref, near_ref, far_ref, weight_ref, *rest):
    outs, rows = rest[-groups - 1 : -1], rest[-1]
    part = near_ref.shape[0] // groups

    @pl.when(pl.program_id(0) == 0)
    def _():
        for flip in range(groups):
            at = pl.multiple_of((place_ref[0] ^ flip) * part, part)
            low = flip * CORES * part
            rows[low : low + part] = near_ref[pl.ds(at, part)]
            rows[low + part : low + 2 * part] = far_ref[pl.ds(at, part)]

    full = dot(rows[...], weight_ref[...], CONTRACT_LAST).astype(jnp.bfloat16)
    for flip in range(groups):
        for core in range(CORES):
            low = (flip * CORES + core) * part
            outs[flip][core] = full[low : low + part]


def chunk_product(near, far, weight, group, groups, *gates):
    block, depth = near.shape
    width = weight.shape[0]
    tile = tile_of(width)
    part = block // groups
    return pl.pallas_call(
        functools.partial(chunk_kernel, groups),
        grid_spec=pltpu.PrefetchScalarGridSpec(
            num_scalar_prefetch=1,
            grid=(width // tile,),
            in_specs=[
                pl.BlockSpec((block, depth), lambda at, place: (0, 0)),
                pl.BlockSpec((block, depth), lambda at, place: (0, 0)),
                pl.BlockSpec((tile, depth), lambda at, place: (at, 0)),
            ]
            + [ANYWHERE] * len(gates),
            out_specs=[pl.BlockSpec((CORES, part, tile), lambda at, place: (0, 0, at))] * groups,
            scratch_shapes=[pltpu.VMEM((CORES * block, depth), jnp.bfloat16)],
        ),
        out_shape=[jax.ShapeDtypeStruct((CORES, part, width), jnp.bfloat16)] * groups,
        compiler_params=pltpu.CompilerParams(vmem_limit_bytes=24 << 20),
        cost_estimate=pl.CostEstimate(
            flops=2 * CORES * block * depth * width,
            bytes_accessed=2 * (width * depth + CORES * block * (depth + width)),
            transcendentals=0,
        ),
    )(group.reshape(1), near, far, weight, *gates)


def join_kernel(groups, slab, place_ref, *refs):
    bases, term_ref, out_ref = refs[:groups], refs[groups], refs[groups + 1]
    width = bases[0].shape[2]
    for flip in range(groups):

        @pl.when(pl.program_id(0) == flip)
        def _():
            for at in range(term_ref.shape[0]):
                low = at * slab
                base = bases[flip][low // width, :, low % width : low % width + slab]
                total = base.astype(jnp.float32) + term_ref[at].astype(jnp.float32)
                out_ref[:, low : low + slab] = total.astype(jnp.bfloat16)


def join(bases, term, group):
    groups = len(bases)
    each, part, width = bases[0].shape
    count, block, slab = term.shape
    if slab % 128:
        base = jnp.zeros((groups, part, each, width), jnp.bfloat16)
        for flip, rows in enumerate(bases):
            base = lax.dynamic_update_index_in_dim(base, rows.transpose(1, 0, 2), group ^ flip, 0)
        total = base.reshape(block, -1).astype(jnp.float32)
        return (total + term.transpose(1, 0, 2).reshape(block, -1)).astype(jnp.bfloat16)
    return pl.pallas_call(
        functools.partial(join_kernel, groups, slab),
        grid_spec=pltpu.PrefetchScalarGridSpec(
            num_scalar_prefetch=1,
            grid=(groups,),
            in_specs=[pl.BlockSpec((each, part, width), lambda at, place: (0, 0, 0))] * groups
            + [pl.BlockSpec((count, part, slab), lambda at, place: (0, place[0] ^ at, 0))],
            out_specs=pl.BlockSpec((part, each * width), lambda at, place: (place[0] ^ at, 0)),
        ),
        out_shape=jax.ShapeDtypeStruct((block, each * width), jnp.bfloat16),
        compiler_params=pltpu.CompilerParams(vmem_limit_bytes=24 << 20),
        cost_estimate=pl.CostEstimate(
            flops=block * each * width, bytes_accessed=6 * block * each * width, transcendentals=0
        ),
    )(group.reshape(1), *bases, term)


def add(*terms):
    return sum(term.astype(jnp.float32) for term in terms).astype(jnp.bfloat16)


def touch_kernel(*refs):
    pass


def touch(values, *gates):
    return pl.pallas_call(
        touch_kernel,
        in_specs=[ANYWHERE] * (len(values) + len(gates)),
        out_specs=[ANYWHERE] * len(values),
        out_shape=[jax.ShapeDtypeStruct(value.shape, value.dtype) for value in values],
        input_output_aliases={at: at for at in range(len(values))},
        compiler_params=pltpu.CompilerParams(vmem_limit_bytes=1 << 20),
    )(*values, *gates)


def after(value, *others):
    return lax.optimization_barrier((value,) + others)[0]


def project(rows, adapter, mask):
    tenants, ranks, width = adapter.shape
    flat = adapter.reshape(tenants * ranks, width)
    parts = []
    for at, size in pieces(rows.shape[0]):
        full = dot(rows[at : at + size], flat, CONTRACT_LAST)
        chosen = full.reshape(size, tenants, ranks) * mask[at : at + size, :, None]
        parts.append(jnp.sum(chosen, axis=1))
    return jnp.concatenate(parts, axis=0).astype(jnp.bfloat16)


def project_kernel(owner_ref, grad_ref, act_ref, up_ref, down_ref, out_ref):
    rows, lanes = out_ref.shape
    owner = owner_ref[...]
    lane = lax.broadcasted_iota(jnp.int32, (rows, lanes), 1)
    high = (lane >= lanes // 2).astype(jnp.int32)

    def pick(left, adapter):
        full = dot(left, adapter, CONTRACT_LAST)
        total = jnp.zeros((rows, lanes), jnp.float32)
        for pair in range(full.shape[1] // lanes):
            mine = owner == 2 * pair + high
            total += jnp.where(mine, full[:, pair * lanes : (pair + 1) * lanes], 0.0)
        return total + pltpu.roll(total, lanes // 2, 1)

    grad = pick(grad_ref[...], up_ref[...])
    act = pick(act_ref[...], down_ref[...])
    out_ref[...] = jnp.where(high == 0, grad, act).astype(jnp.bfloat16)


def project_both(grad_slab, hidden_slab, adapter_up, adapter_down, owner, mask):
    tenants, ranks, up_slab = adapter_up.shape
    down_slab = adapter_down.shape[2]
    tokens = grad_slab.shape[0]
    rows = 256
    if up_slab % 128 or down_slab % 128 or ranks != 64 or tenants % 2 or tokens % rows:
        return jnp.concatenate(
            [project(grad_slab, adapter_up, mask), project(hidden_slab, adapter_down, mask)], axis=1
        )
    return pl.pallas_call(
        project_kernel,
        grid=(tokens // rows,),
        in_specs=[
            pl.BlockSpec((rows, 1), lambda at: (at, 0)),
            pl.BlockSpec((rows, up_slab), lambda at: (at, 0)),
            pl.BlockSpec((rows, down_slab), lambda at: (at, 0)),
            pl.BlockSpec((tenants * ranks, up_slab), lambda at: (0, 0)),
            pl.BlockSpec((tenants * ranks, down_slab), lambda at: (0, 0)),
        ],
        out_specs=pl.BlockSpec((rows, 2 * ranks), lambda at: (at, 0)),
        out_shape=jax.ShapeDtypeStruct((tokens, 2 * ranks), jnp.bfloat16),
        compiler_params=pltpu.CompilerParams(vmem_limit_bytes=24 << 20),
        cost_estimate=pl.CostEstimate(
            flops=2 * tokens * tenants * ranks * (up_slab + down_slab),
            bytes_accessed=2 * (tokens + tenants * ranks) * (up_slab + down_slab),
            transcendentals=0,
        ),
    )(
        owner.reshape(tokens, 1),
        grad_slab,
        hidden_slab,
        adapter_up.reshape(tenants * ranks, up_slab),
        adapter_down.reshape(tenants * ranks, down_slab),
    )


def spread(rank, mask):
    wide = rank[:, None, :] * mask.astype(jnp.bfloat16)[:, :, None]
    return wide.reshape(rank.shape[0], -1)


def adapter_grad(rank, mask, rows, weights):
    tenants, ranks = mask.shape[1], rank.shape[1]
    parts = []
    for at, size in pieces(tenants * ranks):
        low, high = at // ranks, (at + size) // ranks
        grad = dot(spread(rank, mask[:, low:high]), rows, CONTRACT_ROWS)
        parts.append(grad.reshape(high - low, ranks, -1) * weights[low:high, None, None])
    return jnp.concatenate(parts, axis=0)


def shards(grad_output, hidden, down_weight, adapter_down, adapter_up, job_tenant, job_count):
    index = lax.axis_index("seq")
    group = lax.axis_index("grp")
    count = lax.axis_size("seq")
    groups = lax.axis_size("grp")
    chips = count // CORES
    chip, core = index // CORES, index % CORES
    block = grad_output.shape[0]
    tenants, ranks, down_slab = adapter_down.shape
    up_slab = adapter_up.shape[2]
    width = down_weight.shape[0]
    part = block // groups

    named = (job_tenant[:, :, None] == jnp.arange(tenants, dtype=jnp.int32)).astype(jnp.float32)
    totals = jnp.sum(job_count.astype(jnp.float32)[:, :, None] * named, axis=(0, 1))
    weights = ADAPTER_SCALE / totals
    ends = jnp.cumsum(job_count, axis=1)
    places = jnp.arange(block, dtype=jnp.int32)[None, :, None]
    member = (places >= (ends - job_count)[:, None, :]) & (places < ends[:, None, :])
    owner = jnp.sum(jnp.where(member, job_tenant[:, None, :], 0), axis=2).reshape(count * block)
    mask = (owner[:, None] == jnp.arange(tenants, dtype=jnp.int32)).astype(jnp.float32)

    def seq_move(value, chips_back, flip):
        pairs = [
            (s, ((s // CORES - chips_back) % chips) * CORES + ((s % CORES) ^ flip))
            for s in range(count)
        ]
        return lax.ppermute(value, "seq", pairs)

    def grp_move(value, flip):
        return lax.ppermute(value, "grp", [(g, g ^ flip) for g in range(groups)])

    held = [grad_output]
    for step in range(1, chips):
        held.append(seq_move(held[-1], -1, 0))
    pairs = [(near, seq_move(near, 0, 1)) for near in held]

    hidden_slab = lax.all_to_all(
        hidden.reshape(block, count, down_slab).transpose(1, 0, 2),
        "seq",
        split_axis=0,
        concat_axis=0,
        tiled=True,
    ).reshape(count * block, down_slab)

    last = chips - 1
    grad_slab = jnp.zeros((count, block, up_slab), jnp.bfloat16)
    for step, pair in enumerate(pairs):
        back = ((chip - step) % chips) * CORES
        for flip, rows in enumerate(pair):
            columns = lax.dynamic_slice_in_dim(rows, index * up_slab, up_slab, 1)
            grad_slab = lax.dynamic_update_index_in_dim(grad_slab, columns, back + (core ^ flip), 0)
    grad_slab = grad_slab.reshape(count * block, up_slab)
    ranked = project_both(grad_slab, hidden_slab, adapter_up, adapter_down, owner, mask)

    products = [
        chunk_product(near, far, down_weight, group, groups, *([ranked] if step == last else []))
        for step, (near, far) in enumerate(pairs)
    ]
    came = []
    for step in range(chips):
        kept = products[step][0]
        others = [grp_move(products[step][flip], flip) for flip in range(1, groups)]
        gates = [products[step + 1][0]] if step < last else []
        if gates:
            (others[0],) = touch([others[0]], *gates)
        sums = add(kept, *others)
        came.append(seq_move(sums, step, 0) if step else sums)

    devices = count * groups
    share = lax.all_to_all(
        ranked.reshape(devices, -1, 2 * ranks),
        ("grp", "seq"),
        split_axis=0,
        concat_axis=0,
        tiled=True,
    )
    share = jnp.sum(share.astype(jnp.float32), axis=0).astype(jnp.bfloat16)
    ranked = lax.all_to_all(
        jnp.broadcast_to(share[None], (devices,) + share.shape),
        ("grp", "seq"),
        split_axis=0,
        concat_axis=0,
        tiled=True,
    ).reshape(count * block, 2 * ranks)
    (ranked,) = touch([ranked], sums)
    grad_rank = ranked[:, :ranks]

    flat_down = adapter_down.reshape(tenants * ranks, down_slab)
    term = jnp.concatenate(
        [
            jnp.dot(
                spread(grad_rank[at : at + size], mask[at : at + size]),
                flat_down,
                preferred_element_type=jnp.float32,
            )
            for at, size in pieces(count * block)
        ],
        axis=0,
    )
    term = (term * ADAPTER_SCALE).astype(jnp.bfloat16).reshape(count, block, down_slab)
    rank_here = after(ranked, term)
    term = lax.all_to_all(term, "seq", split_axis=0, concat_axis=0, tiled=True)

    mine = jnp.stack([sums[0] for sums in came])
    theirs = seq_move(jnp.stack([sums[1] for sums in came]), 0, 1)
    halves = jnp.stack([mine, theirs], axis=1).reshape(count, part, width)

    each = count // groups
    bases = []
    for flip in range(groups):
        wanted = []
        for at in range(each):
            owner_at = (group ^ flip) * each + at
            ahead = (owner_at // CORES - chip) % chips
            wanted.append(
                lax.dynamic_slice_in_dim(halves, ahead * CORES + (owner_at % CORES ^ core), 1, 0)
            )
        sums = jnp.concatenate(wanted, axis=0)
        bases.append(grp_move(sums, flip) if flip else sums)

    grad_down = adapter_grad(rank_here[:, :ranks], mask, hidden_slab, weights)
    grad_up = adapter_grad(rank_here[:, ranks:], mask, grad_slab, weights)
    grad_hidden = join(bases, term, group)
    return grad_hidden, grad_down, grad_up


def solution(mesh):
    placed = (
        P("seq", "grp"),
        P("seq", "grp"),
        P("seq", "grp"),
        P(None, None, ("grp", "seq")),
        P(None, None, ("grp", "seq")),
        P(),
        P(),
    )
    return jax.shard_map(
        shards,
        mesh=mesh,
        in_specs=placed,
        out_specs=(P("seq", "grp"), P(None, None, ("grp", "seq")), P(None, None, ("grp", "seq"))),
        check_vma=False,
    )
```

```python
import functools

import jax
import jax.numpy as jnp
from jax import lax
from jax.experimental import pallas as pl
from jax.experimental.pallas import tpu as pltpu
from jax.sharding import PartitionSpec as P

ADAPTER_SCALE = 2.0
CONTRACT_LAST = (((1,), (1,)), ((), ()))
CONTRACT_ROWS = (((0,), (0,)), ((), ()))
CORES = 2
MOST_ROWS = 1024
ANYWHERE = pl.BlockSpec(memory_space=pl.ANY)


def dot(left, right, dims):
    return lax.dot_general(left, right, dims, preferred_element_type=jnp.float32)


def pieces(total):
    step = min(total, MOST_ROWS)
    return [(at, min(step, total - at)) for at in range(0, total, step)]


def tile_of(width):
    fits = [tile for tile in (512, 448, 384, 256, 128) if width % tile == 0 and tile % 128 == 0]
    return fits[0] if fits else width


def chunk_kernel(groups, place_ref, near_ref, far_ref, weight_ref, *rest):
    outs, rows = rest[-groups - 1 : -1], rest[-1]
    part = near_ref.shape[0] // groups

    @pl.when(pl.program_id(0) == 0)
    def _():
        for flip in range(groups):
            at = pl.multiple_of((place_ref[0] ^ flip) * part, part)
            low = flip * CORES * part
            rows[low : low + part] = near_ref[pl.ds(at, part)]
            rows[low + part : low + 2 * part] = far_ref[pl.ds(at, part)]

    full = dot(rows[...], weight_ref[...], CONTRACT_LAST).astype(jnp.bfloat16)
    for flip in range(groups):
        for core in range(CORES):
            low = (flip * CORES + core) * part
            outs[flip][core] = full[low : low + part]


def chunk_product(near, far, weight, group, groups, *gates):
    block, depth = near.shape
    width = weight.shape[0]
    tile = tile_of(width)
    part = block // groups
    return pl.pallas_call(
        functools.partial(chunk_kernel, groups),
        grid_spec=pltpu.PrefetchScalarGridSpec(
            num_scalar_prefetch=1,
            grid=(width // tile,),
            in_specs=[
                pl.BlockSpec((block, depth), lambda at, place: (0, 0)),
                pl.BlockSpec((block, depth), lambda at, place: (0, 0)),
                pl.BlockSpec((tile, depth), lambda at, place: (at, 0)),
            ]
            + [ANYWHERE] * len(gates),
            out_specs=[pl.BlockSpec((CORES, part, tile), lambda at, place: (0, 0, at))] * groups,
            scratch_shapes=[pltpu.VMEM((CORES * block, depth), jnp.bfloat16)],
        ),
        out_shape=[jax.ShapeDtypeStruct((CORES, part, width), jnp.bfloat16)] * groups,
        compiler_params=pltpu.CompilerParams(vmem_limit_bytes=24 << 20),
        cost_estimate=pl.CostEstimate(
            flops=2 * CORES * block * depth * width,
            bytes_accessed=2 * (width * depth + CORES * block * (depth + width)),
            transcendentals=0,
        ),
    )(group.reshape(1), near, far, weight, *gates)


def join_kernel(groups, slab, place_ref, *refs):
    bases, term_ref, out_ref = refs[:groups], refs[groups], refs[groups + 1]
    width = bases[0].shape[2]
    for flip in range(groups):

        @pl.when(pl.program_id(0) == flip)
        def _():
            for at in range(term_ref.shape[0]):
                low = at * slab
                base = bases[flip][low // width, :, low % width : low % width + slab]
                total = base.astype(jnp.float32) + term_ref[at].astype(jnp.float32)
                out_ref[:, low : low + slab] = total.astype(jnp.bfloat16)


def join(bases, term, group):
    groups = len(bases)
    each, part, width = bases[0].shape
    count, block, slab = term.shape
    if slab % 128:
        base = jnp.zeros((groups, part, each, width), jnp.bfloat16)
        for flip, rows in enumerate(bases):
            base = lax.dynamic_update_index_in_dim(base, rows.transpose(1, 0, 2), group ^ flip, 0)
        total = base.reshape(block, -1).astype(jnp.float32)
        return (total + term.transpose(1, 0, 2).reshape(block, -1)).astype(jnp.bfloat16)
    return pl.pallas_call(
        functools.partial(join_kernel, groups, slab),
        grid_spec=pltpu.PrefetchScalarGridSpec(
            num_scalar_prefetch=1,
            grid=(groups,),
            in_specs=[pl.BlockSpec((each, part, width), lambda at, place: (0, 0, 0))] * groups
            + [pl.BlockSpec((count, part, slab), lambda at, place: (0, place[0] ^ at, 0))],
            out_specs=pl.BlockSpec((part, each * width), lambda at, place: (place[0] ^ at, 0)),
        ),
        out_shape=jax.ShapeDtypeStruct((block, each * width), jnp.bfloat16),
        compiler_params=pltpu.CompilerParams(vmem_limit_bytes=24 << 20),
        cost_estimate=pl.CostEstimate(
            flops=block * each * width, bytes_accessed=6 * block * each * width, transcendentals=0
        ),
    )(group.reshape(1), *bases, term)


def add(*terms):
    return sum(term.astype(jnp.float32) for term in terms).astype(jnp.bfloat16)


def touch_kernel(*refs):
    pass


def touch(values, *gates):
    return pl.pallas_call(
        touch_kernel,
        in_specs=[ANYWHERE] * (len(values) + len(gates)),
        out_specs=[ANYWHERE] * len(values),
        out_shape=[jax.ShapeDtypeStruct(value.shape, value.dtype) for value in values],
        input_output_aliases={at: at for at in range(len(values))},
        compiler_params=pltpu.CompilerParams(vmem_limit_bytes=1 << 20),
    )(*values, *gates)


def after(value, *others):
    return lax.optimization_barrier((value,) + others)[0]


def project(rows, adapter, mask):
    tenants, ranks, width = adapter.shape
    flat = adapter.reshape(tenants * ranks, width)
    parts = []
    for at, size in pieces(rows.shape[0]):
        full = dot(rows[at : at + size], flat, CONTRACT_LAST)
        chosen = full.reshape(size, tenants, ranks) * mask[at : at + size, :, None]
        parts.append(jnp.sum(chosen, axis=1))
    return jnp.concatenate(parts, axis=0).astype(jnp.bfloat16)


def project_kernel(owner_ref, grad_ref, act_ref, up_ref, down_ref, out_ref):
    rows, lanes = out_ref.shape
    owner = owner_ref[...]
    lane = lax.broadcasted_iota(jnp.int32, (rows, lanes), 1)
    high = (lane >= lanes // 2).astype(jnp.int32)

    def pick(left, adapter):
        full = dot(left, adapter, CONTRACT_LAST)
        total = jnp.zeros((rows, lanes), jnp.float32)
        for pair in range(full.shape[1] // lanes):
            mine = owner == 2 * pair + high
            total += jnp.where(mine, full[:, pair * lanes : (pair + 1) * lanes], 0.0)
        return total + pltpu.roll(total, lanes // 2, 1)

    grad = pick(grad_ref[...], up_ref[...])
    act = pick(act_ref[...], down_ref[...])
    out_ref[...] = jnp.where(high == 0, grad, act).astype(jnp.bfloat16)


def project_both(grad_slab, hidden_slab, adapter_up, adapter_down, owner, mask):
    tenants, ranks, up_slab = adapter_up.shape
    down_slab = adapter_down.shape[2]
    tokens = grad_slab.shape[0]
    rows = 256
    if up_slab % 128 or down_slab % 128 or ranks != 64 or tenants % 2 or tokens % rows:
        return jnp.concatenate(
            [project(grad_slab, adapter_up, mask), project(hidden_slab, adapter_down, mask)], axis=1
        )
    return pl.pallas_call(
        project_kernel,
        grid=(tokens // rows,),
        in_specs=[
            pl.BlockSpec((rows, 1), lambda at: (at, 0)),
            pl.BlockSpec((rows, up_slab), lambda at: (at, 0)),
            pl.BlockSpec((rows, down_slab), lambda at: (at, 0)),
            pl.BlockSpec((tenants * ranks, up_slab), lambda at: (0, 0)),
            pl.BlockSpec((tenants * ranks, down_slab), lambda at: (0, 0)),
        ],
        out_specs=pl.BlockSpec((rows, 2 * ranks), lambda at: (at, 0)),
        out_shape=jax.ShapeDtypeStruct((tokens, 2 * ranks), jnp.bfloat16),
        compiler_params=pltpu.CompilerParams(vmem_limit_bytes=56 << 20),
        cost_estimate=pl.CostEstimate(
            flops=2 * tokens * tenants * ranks * (up_slab + down_slab),
            bytes_accessed=2 * (tokens + tenants * ranks) * (up_slab + down_slab),
            transcendentals=0,
        ),
    )(
        owner.reshape(tokens, 1),
        grad_slab,
        hidden_slab,
        adapter_up.reshape(tenants * ranks, up_slab),
        adapter_down.reshape(tenants * ranks, down_slab),
    )


def spread(rank, mask):
    wide = rank[:, None, :] * mask.astype(jnp.bfloat16)[:, :, None]
    return wide.reshape(rank.shape[0], -1)


def adapter_grad(rank, mask, rows, weights):
    tenants, ranks = mask.shape[1], rank.shape[1]
    parts = []
    for at, size in pieces(tenants * ranks):
        low, high = at // ranks, (at + size) // ranks
        grad = dot(spread(rank, mask[:, low:high]), rows, CONTRACT_ROWS)
        parts.append(grad.reshape(high - low, ranks, -1) * weights[low:high, None, None])
    return jnp.concatenate(parts, axis=0)


def shards(grad_output, hidden, down_weight, adapter_down, adapter_up, job_tenant, job_count):
    index = lax.axis_index("seq")
    group = lax.axis_index("grp")
    count = lax.axis_size("seq")
    groups = lax.axis_size("grp")
    chips = count // CORES
    chip, core = index // CORES, index % CORES
    block = grad_output.shape[0]
    tenants, ranks, down_slab = adapter_down.shape
    up_slab = adapter_up.shape[2]
    width = down_weight.shape[0]
    part = block // groups

    named = (job_tenant[:, :, None] == jnp.arange(tenants, dtype=jnp.int32)).astype(jnp.float32)
    totals = jnp.sum(job_count.astype(jnp.float32)[:, :, None] * named, axis=(0, 1))
    weights = ADAPTER_SCALE / totals
    ends = jnp.cumsum(job_count, axis=1)
    places = jnp.arange(block, dtype=jnp.int32)[None, :, None]
    member = (places >= (ends - job_count)[:, None, :]) & (places < ends[:, None, :])
    owner = jnp.sum(jnp.where(member, job_tenant[:, None, :], 0), axis=2).reshape(count * block)
    mask = (owner[:, None] == jnp.arange(tenants, dtype=jnp.int32)).astype(jnp.float32)

    def seq_move(value, chips_back, flip):
        pairs = [
            (s, ((s // CORES - chips_back) % chips) * CORES + ((s % CORES) ^ flip))
            for s in range(count)
        ]
        return lax.ppermute(value, "seq", pairs)

    def grp_move(value, flip):
        return lax.ppermute(value, "grp", [(g, g ^ flip) for g in range(groups)])

    held = [grad_output]
    for step in range(1, chips):
        held.append(seq_move(held[-1], -1, 0))
    pairs = [(near, seq_move(near, 0, 1)) for near in held]

    hidden_slab = lax.all_to_all(
        hidden.reshape(block, count, down_slab).transpose(1, 0, 2),
        "seq",
        split_axis=0,
        concat_axis=0,
        tiled=True,
    ).reshape(count * block, down_slab)

    last = chips - 1
    grad_slab = jnp.zeros((count, block, up_slab), jnp.bfloat16)
    for step, pair in enumerate(pairs):
        back = ((chip - step) % chips) * CORES
        for flip, rows in enumerate(pair):
            columns = lax.dynamic_slice_in_dim(rows, index * up_slab, up_slab, 1)
            grad_slab = lax.dynamic_update_index_in_dim(grad_slab, columns, back + (core ^ flip), 0)
    grad_slab = grad_slab.reshape(count * block, up_slab)
    products = [chunk_product(near, far, down_weight, group, groups) for near, far in pairs]
    (hidden_slab,) = touch([hidden_slab], products[last][0])
    ranked = project_both(grad_slab, hidden_slab, adapter_up, adapter_down, owner, mask)

    devices = count * groups
    share = lax.all_to_all(
        ranked.reshape(devices, -1, 2 * ranks),
        ("grp", "seq"),
        split_axis=0,
        concat_axis=0,
        tiled=True,
    )
    share = jnp.sum(share.astype(jnp.float32), axis=0).astype(jnp.bfloat16)
    rank_sums = lax.all_to_all(
        jnp.broadcast_to(share[None], (devices,) + share.shape),
        ("grp", "seq"),
        split_axis=0,
        concat_axis=0,
        tiled=True,
    ).reshape(count * block, 2 * ranks)

    came = []
    for step in range(chips):
        kept, *sent = products[step]
        if step == last:
            sent = touch(sent, ranked)
        others = [grp_move(rows, flip + 1) for flip, rows in enumerate(sent)]
        if step < last - 1:
            gate = products[step + 1][0]
        else:
            gate = rank_sums if step == last else share
        (others[0],) = touch([others[0]], gate)
        sums = add(kept, *others)
        came.append(seq_move(sums, step, 0) if step else sums)
    (ranked,) = touch([rank_sums], sums)
    grad_rank = ranked[:, :ranks]

    flat_down = adapter_down.reshape(tenants * ranks, down_slab)
    term = jnp.concatenate(
        [
            jnp.dot(
                spread(grad_rank[at : at + size], mask[at : at + size]),
                flat_down,
                preferred_element_type=jnp.float32,
            )
            for at, size in pieces(count * block)
        ],
        axis=0,
    )
    term = (term * ADAPTER_SCALE).astype(jnp.bfloat16).reshape(count, block, down_slab)
    rank_here = after(ranked, term)
    term_here = term
    term = lax.all_to_all(term, "seq", split_axis=0, concat_axis=0, tiled=True)

    came = touch(came, term_here)
    mine = jnp.stack([sums[0] for sums in came])
    theirs = seq_move(jnp.stack([sums[1] for sums in came]), 0, 1)
    halves = jnp.stack([mine, theirs], axis=1).reshape(count, part, width)

    each = count // groups
    bases = []
    for flip in range(groups):
        wanted = []
        for at in range(each):
            owner_at = (group ^ flip) * each + at
            ahead = (owner_at // CORES - chip) % chips
            wanted.append(
                lax.dynamic_slice_in_dim(halves, ahead * CORES + (owner_at % CORES ^ core), 1, 0)
            )
        sums = jnp.concatenate(wanted, axis=0)
        bases.append(grp_move(sums, flip) if flip else sums)

    grad_down = adapter_grad(rank_here[:, :ranks], mask, hidden_slab, weights)
    grad_up = adapter_grad(rank_here[:, ranks:], mask, grad_slab, weights)
    grad_hidden = join(bases, term, group)
    return grad_hidden, grad_down, grad_up


def solution(mesh):
    placed = (
        P("seq", "grp"),
        P("seq", "grp"),
        P("seq", "grp"),
        P(None, None, ("grp", "seq")),
        P(None, None, ("grp", "seq")),
        P(),
        P(),
    )
    return jax.shard_map(
        shards,
        mesh=mesh,
        in_specs=placed,
        out_specs=(P("seq", "grp"), P(None, None, ("grp", "seq")), P(None, None, ("grp", "seq"))),
        check_vma=False,
    )
```

```python
import functools

import jax
import jax.numpy as jnp
from jax import lax
from jax.experimental import pallas as pl
from jax.experimental.pallas import tpu as pltpu
from jax.sharding import PartitionSpec as P

ADAPTER_SCALE = 2.0
CONTRACT_LAST = (((1,), (1,)), ((), ()))
CONTRACT_ROWS = (((0,), (0,)), ((), ()))
CORES = 2
MOST_ROWS = 1024
ANYWHERE = pl.BlockSpec(memory_space=pl.ANY)


def dot(left, right, dims):
    return lax.dot_general(left, right, dims, preferred_element_type=jnp.float32)


def pieces(total):
    step = min(total, MOST_ROWS)
    return [(at, min(step, total - at)) for at in range(0, total, step)]


def tile_of(width):
    fits = [tile for tile in (512, 448, 384, 256, 128) if width % tile == 0 and tile % 128 == 0]
    return fits[0] if fits else width


def chunk_kernel(groups, place_ref, near_ref, far_ref, weight_ref, *rest):
    outs, rows = rest[-groups - 1 : -1], rest[-1]
    part = near_ref.shape[0] // groups

    @pl.when(pl.program_id(0) == 0)
    def _():
        for flip in range(groups):
            at = pl.multiple_of((place_ref[0] ^ flip) * part, part)
            low = flip * CORES * part
            rows[low : low + part] = near_ref[pl.ds(at, part)]
            rows[low + part : low + 2 * part] = far_ref[pl.ds(at, part)]

    full = dot(rows[...], weight_ref[...], CONTRACT_LAST).astype(jnp.bfloat16)
    for flip in range(groups):
        for core in range(CORES):
            low = (flip * CORES + core) * part
            outs[flip][core] = full[low : low + part]


def chunk_product(near, far, weight, group, groups, *gates):
    block, depth = near.shape
    width = weight.shape[0]
    tile = tile_of(width)
    part = block // groups
    return pl.pallas_call(
        functools.partial(chunk_kernel, groups),
        grid_spec=pltpu.PrefetchScalarGridSpec(
            num_scalar_prefetch=1,
            grid=(width // tile,),
            in_specs=[
                pl.BlockSpec((block, depth), lambda at, place: (0, 0)),
                pl.BlockSpec((block, depth), lambda at, place: (0, 0)),
                pl.BlockSpec((tile, depth), lambda at, place: (at, 0)),
            ]
            + [ANYWHERE] * len(gates),
            out_specs=[pl.BlockSpec((CORES, part, tile), lambda at, place: (0, 0, at))] * groups,
            scratch_shapes=[pltpu.VMEM((CORES * block, depth), jnp.bfloat16)],
        ),
        out_shape=[jax.ShapeDtypeStruct((CORES, part, width), jnp.bfloat16)] * groups,
        compiler_params=pltpu.CompilerParams(vmem_limit_bytes=24 << 20),
        cost_estimate=pl.CostEstimate(
            flops=2 * CORES * block * depth * width,
            bytes_accessed=2 * (width * depth + CORES * block * (depth + width)),
            transcendentals=0,
        ),
    )(group.reshape(1), near, far, weight, *gates)


def join_kernel(groups, slab, place_ref, *refs):
    bases, term_ref, out_ref = refs[:groups], refs[groups], refs[groups + 1]
    width = bases[0].shape[2]
    for flip in range(groups):

        @pl.when(pl.program_id(0) == flip)
        def _():
            for at in range(term_ref.shape[0]):
                low = at * slab
                base = bases[flip][low // width, :, low % width : low % width + slab]
                total = base.astype(jnp.float32) + term_ref[at].astype(jnp.float32)
                out_ref[:, low : low + slab] = total.astype(jnp.bfloat16)


def join(bases, term, group):
    groups = len(bases)
    each, part, width = bases[0].shape
    count, block, slab = term.shape
    if slab % 128:
        base = jnp.zeros((groups, part, each, width), jnp.bfloat16)
        for flip, rows in enumerate(bases):
            base = lax.dynamic_update_index_in_dim(base, rows.transpose(1, 0, 2), group ^ flip, 0)
        total = base.reshape(block, -1).astype(jnp.float32)
        return (total + term.transpose(1, 0, 2).reshape(block, -1)).astype(jnp.bfloat16)
    return pl.pallas_call(
        functools.partial(join_kernel, groups, slab),
        grid_spec=pltpu.PrefetchScalarGridSpec(
            num_scalar_prefetch=1,
            grid=(groups,),
            in_specs=[pl.BlockSpec((each, part, width), lambda at, place: (0, 0, 0))] * groups
            + [pl.BlockSpec((count, part, slab), lambda at, place: (0, place[0] ^ at, 0))],
            out_specs=pl.BlockSpec((part, each * width), lambda at, place: (place[0] ^ at, 0)),
        ),
        out_shape=jax.ShapeDtypeStruct((block, each * width), jnp.bfloat16),
        compiler_params=pltpu.CompilerParams(vmem_limit_bytes=24 << 20),
        cost_estimate=pl.CostEstimate(
            flops=block * each * width, bytes_accessed=6 * block * each * width, transcendentals=0
        ),
    )(group.reshape(1), *bases, term)


def add(*terms):
    return sum(term.astype(jnp.float32) for term in terms).astype(jnp.bfloat16)


def touch_kernel(*refs):
    pass


def touch(values, *gates):
    return pl.pallas_call(
        touch_kernel,
        in_specs=[ANYWHERE] * (len(values) + len(gates)),
        out_specs=[ANYWHERE] * len(values),
        out_shape=[jax.ShapeDtypeStruct(value.shape, value.dtype) for value in values],
        input_output_aliases={at: at for at in range(len(values))},
        compiler_params=pltpu.CompilerParams(vmem_limit_bytes=1 << 20),
    )(*values, *gates)


def after(value, *others):
    return lax.optimization_barrier((value,) + others)[0]


def project(rows, adapter, mask):
    tenants, ranks, width = adapter.shape
    flat = adapter.reshape(tenants * ranks, width)
    parts = []
    for at, size in pieces(rows.shape[0]):
        full = dot(rows[at : at + size], flat, CONTRACT_LAST)
        chosen = full.reshape(size, tenants, ranks) * mask[at : at + size, :, None]
        parts.append(jnp.sum(chosen, axis=1))
    return jnp.concatenate(parts, axis=0).astype(jnp.bfloat16)


def project_kernel(owner_ref, grad_ref, act_ref, up_ref, down_ref, out_ref):
    rows, lanes = out_ref.shape
    owner = owner_ref[...]
    lane = lax.broadcasted_iota(jnp.int32, (rows, lanes), 1)
    high = (lane >= lanes // 2).astype(jnp.int32)

    def pick(left, adapter):
        full = dot(left, adapter, CONTRACT_LAST)
        total = jnp.zeros((rows, lanes), jnp.float32)
        for pair in range(full.shape[1] // lanes):
            mine = owner == 2 * pair + high
            total += jnp.where(mine, full[:, pair * lanes : (pair + 1) * lanes], 0.0)
        return total + pltpu.roll(total, lanes // 2, 1)

    grad = pick(grad_ref[...], up_ref[...])
    act = pick(act_ref[...], down_ref[...])
    out_ref[...] = jnp.where(high == 0, grad, act).astype(jnp.bfloat16)


def project_both(grad_slab, hidden_slab, adapter_up, adapter_down, owner, mask):
    tenants, ranks, up_slab = adapter_up.shape
    down_slab = adapter_down.shape[2]
    tokens = grad_slab.shape[0]
    rows = 256
    if up_slab % 128 or down_slab % 128 or ranks != 64 or tenants % 2 or tokens % rows:
        return jnp.concatenate(
            [project(grad_slab, adapter_up, mask), project(hidden_slab, adapter_down, mask)], axis=1
        )
    return pl.pallas_call(
        project_kernel,
        grid=(tokens // rows,),
        in_specs=[
            pl.BlockSpec((rows, 1), lambda at: (at, 0)),
            pl.BlockSpec((rows, up_slab), lambda at: (at, 0)),
            pl.BlockSpec((rows, down_slab), lambda at: (at, 0)),
            pl.BlockSpec((tenants * ranks, up_slab), lambda at: (0, 0)),
            pl.BlockSpec((tenants * ranks, down_slab), lambda at: (0, 0)),
        ],
        out_specs=pl.BlockSpec((rows, 2 * ranks), lambda at: (at, 0)),
        out_shape=jax.ShapeDtypeStruct((tokens, 2 * ranks), jnp.bfloat16),
        compiler_params=pltpu.CompilerParams(vmem_limit_bytes=56 << 20),
        cost_estimate=pl.CostEstimate(
            flops=2 * tokens * tenants * ranks * (up_slab + down_slab),
            bytes_accessed=2 * (tokens + tenants * ranks) * (up_slab + down_slab),
            transcendentals=0,
        ),
    )(
        owner.reshape(tokens, 1),
        grad_slab,
        hidden_slab,
        adapter_up.reshape(tenants * ranks, up_slab),
        adapter_down.reshape(tenants * ranks, down_slab),
    )


def spread(rank, mask):
    wide = rank[:, None, :] * mask.astype(jnp.bfloat16)[:, :, None]
    return wide.reshape(rank.shape[0], -1)


def adapter_grad(rank, mask, rows, weights):
    tenants, ranks = mask.shape[1], rank.shape[1]
    parts = []
    for at, size in pieces(tenants * ranks):
        low, high = at // ranks, (at + size) // ranks
        grad = dot(spread(rank, mask[:, low:high]), rows, CONTRACT_ROWS)
        parts.append(grad.reshape(high - low, ranks, -1) * weights[low:high, None, None])
    return jnp.concatenate(parts, axis=0)


def shards(grad_output, hidden, down_weight, adapter_down, adapter_up, job_tenant, job_count):
    index = lax.axis_index("seq")
    group = lax.axis_index("grp")
    count = lax.axis_size("seq")
    groups = lax.axis_size("grp")
    chips = count // CORES
    chip, core = index // CORES, index % CORES
    block = grad_output.shape[0]
    tenants, ranks, down_slab = adapter_down.shape
    up_slab = adapter_up.shape[2]
    width = down_weight.shape[0]
    part = block // groups

    named = (job_tenant[:, :, None] == jnp.arange(tenants, dtype=jnp.int32)).astype(jnp.float32)
    totals = jnp.sum(job_count.astype(jnp.float32)[:, :, None] * named, axis=(0, 1))
    weights = ADAPTER_SCALE / totals
    ends = jnp.cumsum(job_count, axis=1)
    places = jnp.arange(block, dtype=jnp.int32)[None, :, None]
    member = (places >= (ends - job_count)[:, None, :]) & (places < ends[:, None, :])
    owner = jnp.sum(jnp.where(member, job_tenant[:, None, :], 0), axis=2).reshape(count * block)
    mask = (owner[:, None] == jnp.arange(tenants, dtype=jnp.int32)).astype(jnp.float32)

    def seq_move(value, chips_back, flip):
        pairs = [
            (s, ((s // CORES - chips_back) % chips) * CORES + ((s % CORES) ^ flip))
            for s in range(count)
        ]
        return lax.ppermute(value, "seq", pairs)

    def grp_move(value, flip):
        return lax.ppermute(value, "grp", [(g, g ^ flip) for g in range(groups)])

    last = chips - 1

    def product(step, *gates):
        return chunk_product(*pairs[step], down_weight, group, groups, *gates)

    held, pairs, products = [grad_output], [], []
    for step in range(chips):
        if step:
            held.append(seq_move(held[-1], -1, 0))
        if step == last:
            held[-1:] = touch(held[-1:], products[-1][0])
        pairs.append((held[step], seq_move(held[step], 0, 1)))
        if step < last:
            products.append(product(step))

    hidden_slab = lax.all_to_all(
        hidden.reshape(block, count, down_slab).transpose(1, 0, 2),
        "seq",
        split_axis=0,
        concat_axis=0,
        tiled=True,
    ).reshape(count * block, down_slab)

    came = []

    def sum_up(step, gate, sent):
        others = [grp_move(rows, flip + 1) for flip, rows in enumerate(sent)]
        (others[0],) = touch([others[0]], gate)
        sums = add(products[step][0], *others)
        came.append(seq_move(sums, step, 0) if step else sums)
        return sums

    for step in range(last - 1):
        sums = sum_up(step, products[step + 1][0], products[step][1:])
    products.append(product(last, sums))

    grad_slab = jnp.zeros((count, block, up_slab), jnp.bfloat16)
    for step, pair in enumerate(pairs):
        back = ((chip - step) % chips) * CORES
        for flip, rows in enumerate(pair):
            columns = lax.dynamic_slice_in_dim(rows, index * up_slab, up_slab, 1)
            grad_slab = lax.dynamic_update_index_in_dim(grad_slab, columns, back + (core ^ flip), 0)
    grad_slab = grad_slab.reshape(count * block, up_slab)
    (hidden_slab,) = touch([hidden_slab], products[last][0])
    ranked = project_both(grad_slab, hidden_slab, adapter_up, adapter_down, owner, mask)

    devices = count * groups
    share = lax.all_to_all(
        ranked.reshape(devices, -1, 2 * ranks),
        ("grp", "seq"),
        split_axis=0,
        concat_axis=0,
        tiled=True,
    )
    share = jnp.sum(share.astype(jnp.float32), axis=0).astype(jnp.bfloat16)
    rank_sums = lax.all_to_all(
        jnp.broadcast_to(share[None], (devices,) + share.shape),
        ("grp", "seq"),
        split_axis=0,
        concat_axis=0,
        tiled=True,
    ).reshape(count * block, 2 * ranks)

    sum_up(last - 1, ranked, products[last - 1][1:])
    sums = sum_up(last, rank_sums, touch(products[last][1:], ranked))
    (ranked,) = touch([rank_sums], sums)
    grad_rank = ranked[:, :ranks]

    flat_down = adapter_down.reshape(tenants * ranks, down_slab)
    term = jnp.concatenate(
        [
            jnp.dot(
                spread(grad_rank[at : at + size], mask[at : at + size]),
                flat_down,
                preferred_element_type=jnp.float32,
            )
            for at, size in pieces(count * block)
        ],
        axis=0,
    )
    term = (term * ADAPTER_SCALE).astype(jnp.bfloat16).reshape(count, block, down_slab)
    rank_here = after(ranked, term)
    term_here = term
    term = lax.all_to_all(term, "seq", split_axis=0, concat_axis=0, tiled=True)

    came = touch(came, term_here)
    mine = jnp.stack([sums[0] for sums in came])
    theirs = seq_move(jnp.stack([sums[1] for sums in came]), 0, 1)
    halves = jnp.stack([mine, theirs], axis=1).reshape(count, part, width)

    each = count // groups
    bases = []
    for flip in range(groups):
        wanted = []
        for at in range(each):
            owner_at = (group ^ flip) * each + at
            ahead = (owner_at // CORES - chip) % chips
            wanted.append(
                lax.dynamic_slice_in_dim(halves, ahead * CORES + (owner_at % CORES ^ core), 1, 0)
            )
        sums = jnp.concatenate(wanted, axis=0)
        bases.append(grp_move(sums, flip) if flip else sums)

    grad_down = adapter_grad(rank_here[:, :ranks], mask, hidden_slab, weights)
    grad_up = adapter_grad(rank_here[:, ranks:], mask, grad_slab, weights)
    grad_hidden = join(bases, term, group)
    return grad_hidden, grad_down, grad_up


def solution(mesh):
    placed = (
        P("seq", "grp"),
        P("seq", "grp"),
        P("seq", "grp"),
        P(None, None, ("grp", "seq")),
        P(None, None, ("grp", "seq")),
        P(),
        P(),
    )
    return jax.shard_map(
        shards,
        mesh=mesh,
        in_specs=placed,
        out_specs=(P("seq", "grp"), P(None, None, ("grp", "seq")), P(None, None, ("grp", "seq"))),
        check_vma=False,
    )
```

```python
import functools

import jax
import jax.numpy as jnp
from jax import lax
from jax.experimental import pallas as pl
from jax.experimental.pallas import tpu as pltpu
from jax.sharding import PartitionSpec as P

ADAPTER_SCALE = 2.0
CONTRACT_LAST = (((1,), (1,)), ((), ()))
CONTRACT_ROWS = (((0,), (0,)), ((), ()))
CORES = 2
MOST_ROWS = 1024
ANYWHERE = pl.BlockSpec(memory_space=pl.ANY)


def dot(left, right, dims):
    return lax.dot_general(left, right, dims, preferred_element_type=jnp.float32)


def pieces(total):
    step = min(total, MOST_ROWS)
    return [(at, min(step, total - at)) for at in range(0, total, step)]


def tile_of(width):
    fits = [tile for tile in (512, 448, 384, 256, 128) if width % tile == 0 and tile % 128 == 0]
    return fits[0] if fits else width


def chunk_kernel(stages, place_ref, near_ref, far_ref, weight_ref, *rest):
    outs, rows = rest[:-1], rest[-1]
    part = near_ref.shape[0] // (2 * len(stages))
    sides = [(ref, flips) for ref, order in zip((near_ref, far_ref), stages) for flips in order]
    cuts = [(ref, flip) for ref, flips in sides for flip in flips]

    @pl.when(pl.program_id(0) == 0)
    def _():
        for at, (ref, flip) in enumerate(cuts):
            low = pl.multiple_of((place_ref[0] ^ flip) * part, part)
            rows[at * part : (at + 1) * part] = ref[pl.ds(low, part)]

    full = dot(rows[...], weight_ref[...], CONTRACT_LAST).astype(jnp.bfloat16)
    for at in range(len(cuts)):
        outs[at // 2][at % 2] = full[at * part : (at + 1) * part]


STAGES = (((0, 2), (1, 3)), ((0, 1), (2, 3)))


def chunk_product(near, far, weight, group):
    block, depth = near.shape
    width = weight.shape[0]
    tile = tile_of(width)
    part = block // (2 * len(STAGES))
    return pl.pallas_call(
        functools.partial(chunk_kernel, STAGES),
        grid_spec=pltpu.PrefetchScalarGridSpec(
            num_scalar_prefetch=1,
            grid=(width // tile,),
            in_specs=[
                pl.BlockSpec((block, depth), lambda at, place: (0, 0)),
                pl.BlockSpec((block, depth), lambda at, place: (0, 0)),
                pl.BlockSpec((tile, depth), lambda at, place: (at, 0)),
            ],
            out_specs=[pl.BlockSpec((2, part, tile), lambda at, place: (0, 0, at))] * 4,
            scratch_shapes=[pltpu.VMEM((CORES * block, depth), jnp.bfloat16)],
        ),
        out_shape=[jax.ShapeDtypeStruct((2, part, width), jnp.bfloat16)] * 4,
        compiler_params=pltpu.CompilerParams(vmem_limit_bytes=24 << 20),
        cost_estimate=pl.CostEstimate(
            flops=2 * CORES * block * depth * width,
            bytes_accessed=2 * (width * depth + CORES * block * (depth + width)),
            transcendentals=0,
        ),
    )(group.reshape(1), near, far, weight)


def join_kernel(groups, slab, place_ref, *refs):
    bases, term_ref, out_ref = refs[:groups], refs[groups], refs[groups + 1]
    width = bases[0].shape[2]
    for flip in range(groups):

        @pl.when(pl.program_id(0) == flip)
        def _():
            for at in range(term_ref.shape[0]):
                low = at * slab
                base = bases[flip][low // width, :, low % width : low % width + slab]
                total = base.astype(jnp.float32) + term_ref[at].astype(jnp.float32)
                out_ref[:, low : low + slab] = total.astype(jnp.bfloat16)


def join(bases, term, group):
    groups = len(bases)
    each, part, width = bases[0].shape
    count, block, slab = term.shape
    if slab % 128:
        base = jnp.zeros((groups, part, each, width), jnp.bfloat16)
        for flip, rows in enumerate(bases):
            base = lax.dynamic_update_index_in_dim(base, rows.transpose(1, 0, 2), group ^ flip, 0)
        total = base.reshape(block, -1).astype(jnp.float32)
        return (total + term.transpose(1, 0, 2).reshape(block, -1)).astype(jnp.bfloat16)
    return pl.pallas_call(
        functools.partial(join_kernel, groups, slab),
        grid_spec=pltpu.PrefetchScalarGridSpec(
            num_scalar_prefetch=1,
            grid=(groups,),
            in_specs=[pl.BlockSpec((each, part, width), lambda at, place: (0, 0, 0))] * groups
            + [pl.BlockSpec((count, part, slab), lambda at, place: (0, place[0] ^ at, 0))],
            out_specs=pl.BlockSpec((part, each * width), lambda at, place: (place[0] ^ at, 0)),
        ),
        out_shape=jax.ShapeDtypeStruct((block, each * width), jnp.bfloat16),
        compiler_params=pltpu.CompilerParams(vmem_limit_bytes=24 << 20),
        cost_estimate=pl.CostEstimate(
            flops=block * each * width, bytes_accessed=6 * block * each * width, transcendentals=0
        ),
    )(group.reshape(1), *bases, term)


def add(*terms):
    return sum(term.astype(jnp.float32) for term in terms).astype(jnp.bfloat16)


def touch_kernel(*refs):
    pass


def touch(values, *gates):
    return pl.pallas_call(
        touch_kernel,
        in_specs=[ANYWHERE] * (len(values) + len(gates)),
        out_specs=[ANYWHERE] * len(values),
        out_shape=[jax.ShapeDtypeStruct(value.shape, value.dtype) for value in values],
        input_output_aliases={at: at for at in range(len(values))},
        compiler_params=pltpu.CompilerParams(vmem_limit_bytes=1 << 20),
    )(*values, *gates)


def after(value, *others):
    return lax.optimization_barrier((value,) + others)[0]


def project(rows, adapter, mask):
    tenants, ranks, width = adapter.shape
    flat = adapter.reshape(tenants * ranks, width)
    parts = []
    for at, size in pieces(rows.shape[0]):
        full = dot(rows[at : at + size], flat, CONTRACT_LAST)
        chosen = full.reshape(size, tenants, ranks) * mask[at : at + size, :, None]
        parts.append(jnp.sum(chosen, axis=1))
    return jnp.concatenate(parts, axis=0).astype(jnp.bfloat16)


def spread(rank, mask):
    wide = rank[:, None, :] * mask.astype(jnp.bfloat16)[:, :, None]
    return wide.reshape(rank.shape[0], -1)


def adapter_grad(rank, mask, rows, weights):
    tenants, ranks = mask.shape[1], rank.shape[1]
    parts = []
    for at, size in pieces(tenants * ranks):
        low, high = at // ranks, (at + size) // ranks
        grad = dot(spread(rank, mask[:, low:high]), rows, CONTRACT_ROWS)
        parts.append(grad.reshape(high - low, ranks, -1) * weights[low:high, None, None])
    return jnp.concatenate(parts, axis=0)


def shards(grad_output, hidden, down_weight, adapter_down, adapter_up, job_tenant, job_count):
    index = lax.axis_index("seq")
    group = lax.axis_index("grp")
    count = lax.axis_size("seq")
    groups = lax.axis_size("grp")
    chips = count // CORES
    chip, core = index // CORES, index % CORES
    block = grad_output.shape[0]
    tenants, ranks, down_slab = adapter_down.shape
    up_slab = adapter_up.shape[2]
    width = down_weight.shape[0]
    part = block // groups

    named = (job_tenant[:, :, None] == jnp.arange(tenants, dtype=jnp.int32)).astype(jnp.float32)
    totals = jnp.sum(job_count.astype(jnp.float32)[:, :, None] * named, axis=(0, 1))
    weights = ADAPTER_SCALE / totals
    ends = jnp.cumsum(job_count, axis=1)
    places = jnp.arange(block, dtype=jnp.int32)[None, :, None]
    member = (places >= (ends - job_count)[:, None, :]) & (places < ends[:, None, :])
    owner = jnp.sum(jnp.where(member, job_tenant[:, None, :], 0), axis=2).reshape(count * block)
    mask = (owner[:, None] == jnp.arange(tenants, dtype=jnp.int32)).astype(jnp.float32)

    def seq_move(value, chips_back, flip):
        pairs = [
            (s, ((s // CORES - chips_back) % chips) * CORES + ((s % CORES) ^ flip))
            for s in range(count)
        ]
        return lax.ppermute(value, "seq", pairs)

    def grp_move(value, flip):
        return lax.ppermute(value, "grp", [(g, g ^ flip) for g in range(groups)])

    held = [grad_output]
    for step in range(1, chips):
        held.append(seq_move(held[-1], -1, 0))
    pairs = [(near, seq_move(near, 0, 1)) for near in held]

    hidden_slab = lax.all_to_all(
        hidden.reshape(block, count, down_slab).transpose(1, 0, 2),
        "seq",
        split_axis=0,
        concat_axis=0,
        tiled=True,
    ).reshape(count * block, down_slab)

    last = chips - 1
    products = [chunk_product(near, far, down_weight, group) for near, far in pairs]
    firsts = [
        (grp_move(near_sent, 1), grp_move(far_sent, 2)) for _, near_sent, _, far_sent in products
    ]
    grad_slab = jnp.zeros((count, block, up_slab), jnp.bfloat16)
    for step, pair in enumerate(pairs):
        back = ((chip - step) % chips) * CORES
        for flip, rows in enumerate(pair):
            columns = lax.dynamic_slice_in_dim(rows, index * up_slab, up_slab, 1)
            grad_slab = lax.dynamic_update_index_in_dim(grad_slab, columns, back + (core ^ flip), 0)
    grad_slab = grad_slab.reshape(count * block, up_slab)

    def second(step, *gates):
        near_kept, _, far_kept, _ = products[step]
        near_came, far_came = firsts[step]
        near_came, far_came = lax.optimization_barrier((near_came, far_came) + gates)[:2]
        near_sum = add(near_kept[1], near_came[1])
        far_sum = add(far_kept[1], far_came[1])
        return near_sum, (grp_move(near_sum, 2), grp_move(far_sum, 1))

    def total(step, seconds, *gates):
        near_kept, _, far_kept, _ = products[step]
        near_came, far_came = firsts[step]
        if step == last - 1:
            near_last, far_last = touch(seconds, *gates)
        else:
            near_last, far_last = lax.optimization_barrier(seconds + gates)[:2]
        return (
            add(near_kept[0], near_came[0], near_last),
            add(far_kept[0], far_came[0], far_last),
        )

    arrived = jnp.zeros((count, part, width), jnp.bfloat16)

    def hop(step, sums):
        return [
            sums[flip] if step == 0 and flip == 0 else seq_move(sums[flip], step, flip)
            for flip in range(CORES)
        ]

    def put(arrived, step, came, *gates):
        ahead = ((chip + step) % chips) * CORES
        came = lax.optimization_barrier(tuple(came) + gates)
        for flip in range(CORES):
            arrived = lax.dynamic_update_index_in_dim(arrived, came[flip], ahead + (core ^ flip), 0)
        return arrived

    came = None
    for step in range(last - 1):
        _, seconds = second(step, products[step + 1][0])
        sums = total(step, seconds)
        if came is not None:
            arrived = put(arrived, step - 1, came, sums[0])
        came = hop(step, sums)

    begun, seconds = second(last - 1, products[last][0])
    rows_here = lax.optimization_barrier((grad_slab, hidden_slab, begun))
    ranked = jnp.concatenate(
        [project(rows_here[0], adapter_up, mask), project(rows_here[1], adapter_down, mask)],
        axis=1,
    )
    devices = count * groups
    share = lax.all_to_all(
        ranked.reshape(devices, -1, 2 * ranks),
        ("grp", "seq"),
        split_axis=0,
        concat_axis=0,
        tiled=True,
    )
    sums = total(last - 1, seconds, ranked)
    arrived = put(arrived, last - 2, came, sums[0])
    came = hop(last - 1, sums)
    begun, seconds = second(last, sums[0])
    share = after(share, begun)
    share = jnp.sum(share.astype(jnp.float32), axis=0).astype(jnp.bfloat16)
    ranked = lax.all_to_all(
        jnp.broadcast_to(share[None], (devices,) + share.shape),
        ("grp", "seq"),
        split_axis=0,
        concat_axis=0,
        tiled=True,
    ).reshape(count * block, 2 * ranks)
    sums = total(last, seconds, share)
    arrived = put(arrived, last - 1, came, sums[0])
    came = hop(last, sums)
    ranked = after(ranked, *sums)
    grad_rank = ranked[:, :ranks]

    flat_down = adapter_down.reshape(tenants * ranks, down_slab)
    term = jnp.concatenate(
        [
            jnp.dot(
                spread(grad_rank[at : at + size], mask[at : at + size]),
                flat_down,
                preferred_element_type=jnp.float32,
            )
            for at, size in pieces(count * block)
        ],
        axis=0,
    )
    term = (term * ADAPTER_SCALE).astype(jnp.bfloat16).reshape(count, block, down_slab)
    arrived = put(arrived, last, came, term)
    rank_here = after(ranked, term)
    term = lax.all_to_all(term, "seq", split_axis=0, concat_axis=0, tiled=True)

    each = count // groups
    bases = []
    for flip in range(groups):
        sums = lax.dynamic_slice_in_dim(arrived, (group ^ flip) * each, each, 0)
        bases.append(grp_move(sums, flip) if flip else sums)

    grad_down = adapter_grad(rank_here[:, :ranks], mask, hidden_slab, weights)
    grad_up = adapter_grad(rank_here[:, ranks:], mask, grad_slab, weights)
    grad_hidden = join(bases, term, group)
    return grad_hidden, grad_down, grad_up


def solution(mesh):
    placed = (
        P("seq", "grp"),
        P("seq", "grp"),
        P("seq", "grp"),
        P(None, None, ("grp", "seq")),
        P(None, None, ("grp", "seq")),
        P(),
        P(),
    )
    return jax.shard_map(
        shards,
        mesh=mesh,
        in_specs=placed,
        out_specs=(P("seq", "grp"), P(None, None, ("grp", "seq")), P(None, None, ("grp", "seq"))),
        check_vma=False,
    )
```

```python
import functools

import jax
import jax.numpy as jnp
from jax import lax
from jax.experimental import pallas as pl
from jax.experimental.pallas import tpu as pltpu
from jax.sharding import PartitionSpec as P

ADAPTER_SCALE = 2.0
CONTRACT_LAST = (((1,), (1,)), ((), ()))
CONTRACT_ROWS = (((0,), (0,)), ((), ()))
CORES = 2
MOST_ROWS = 1024
ANYWHERE = pl.BlockSpec(memory_space=pl.ANY)


def dot(left, right, dims):
    return lax.dot_general(left, right, dims, preferred_element_type=jnp.float32)


def pieces(total):
    step = min(total, MOST_ROWS)
    return [(at, min(step, total - at)) for at in range(0, total, step)]


def tile_of(width):
    fits = [tile for tile in (512, 448, 384, 256, 128) if width % tile == 0 and tile % 128 == 0]
    return fits[0] if fits else width


def chunk_kernel(stages, place_ref, near_ref, far_ref, weight_ref, *rest):
    outs, rows = rest[:-1], rest[-1]
    part = near_ref.shape[0] // (2 * len(stages))
    sides = [(ref, flips) for ref, order in zip((near_ref, far_ref), stages) for flips in order]
    cuts = [(ref, flip) for ref, flips in sides for flip in flips]

    @pl.when(pl.program_id(0) == 0)
    def _():
        for at, (ref, flip) in enumerate(cuts):
            low = pl.multiple_of((place_ref[0] ^ flip) * part, part)
            rows[at * part : (at + 1) * part] = ref[pl.ds(low, part)]

    full = dot(rows[...], weight_ref[...], CONTRACT_LAST).astype(jnp.bfloat16)
    for at in range(len(cuts)):
        outs[at // 2][at % 2] = full[at * part : (at + 1) * part]


STAGES = (((0, 2), (1, 3)), ((0, 1), (2, 3)))


def chunk_product(near, far, weight, group):
    block, depth = near.shape
    width = weight.shape[0]
    tile = tile_of(width)
    part = block // (2 * len(STAGES))
    return pl.pallas_call(
        functools.partial(chunk_kernel, STAGES),
        grid_spec=pltpu.PrefetchScalarGridSpec(
            num_scalar_prefetch=1,
            grid=(width // tile,),
            in_specs=[
                pl.BlockSpec((block, depth), lambda at, place: (0, 0)),
                pl.BlockSpec((block, depth), lambda at, place: (0, 0)),
                pl.BlockSpec((tile, depth), lambda at, place: (at, 0)),
            ],
            out_specs=[pl.BlockSpec((2, part, tile), lambda at, place: (0, 0, at))] * 4,
            scratch_shapes=[pltpu.VMEM((CORES * block, depth), jnp.bfloat16)],
        ),
        out_shape=[jax.ShapeDtypeStruct((2, part, width), jnp.bfloat16)] * 4,
        compiler_params=pltpu.CompilerParams(vmem_limit_bytes=24 << 20),
        cost_estimate=pl.CostEstimate(
            flops=2 * CORES * block * depth * width,
            bytes_accessed=2 * (width * depth + CORES * block * (depth + width)),
            transcendentals=0,
        ),
    )(group.reshape(1), near, far, weight)


def join_kernel(groups, slab, place_ref, *refs):
    bases, term_ref, out_ref = refs[:groups], refs[groups], refs[groups + 1]
    width = bases[0].shape[2]
    for flip in range(groups):

        @pl.when(pl.program_id(0) == flip)
        def _():
            for at in range(term_ref.shape[0]):
                low = at * slab
                base = bases[flip][low // width, :, low % width : low % width + slab]
                total = base.astype(jnp.float32) + term_ref[at].astype(jnp.float32)
                out_ref[:, low : low + slab] = total.astype(jnp.bfloat16)


def join(bases, term, group):
    groups = len(bases)
    each, part, width = bases[0].shape
    count, block, slab = term.shape
    if slab % 128:
        base = jnp.zeros((groups, part, each, width), jnp.bfloat16)
        for flip, rows in enumerate(bases):
            base = lax.dynamic_update_index_in_dim(base, rows.transpose(1, 0, 2), group ^ flip, 0)
        total = base.reshape(block, -1).astype(jnp.float32)
        return (total + term.transpose(1, 0, 2).reshape(block, -1)).astype(jnp.bfloat16)
    return pl.pallas_call(
        functools.partial(join_kernel, groups, slab),
        grid_spec=pltpu.PrefetchScalarGridSpec(
            num_scalar_prefetch=1,
            grid=(groups,),
            in_specs=[pl.BlockSpec((each, part, width), lambda at, place: (0, 0, 0))] * groups
            + [pl.BlockSpec((count, part, slab), lambda at, place: (0, place[0] ^ at, 0))],
            out_specs=pl.BlockSpec((part, each * width), lambda at, place: (place[0] ^ at, 0)),
        ),
        out_shape=jax.ShapeDtypeStruct((block, each * width), jnp.bfloat16),
        compiler_params=pltpu.CompilerParams(vmem_limit_bytes=24 << 20),
        cost_estimate=pl.CostEstimate(
            flops=block * each * width, bytes_accessed=6 * block * each * width, transcendentals=0
        ),
    )(group.reshape(1), *bases, term)


def add(*terms):
    return sum(term.astype(jnp.float32) for term in terms).astype(jnp.bfloat16)


def touch_kernel(*refs):
    pass


def touch(values, *gates):
    return pl.pallas_call(
        touch_kernel,
        in_specs=[ANYWHERE] * (len(values) + len(gates)),
        out_specs=[ANYWHERE] * len(values),
        out_shape=[jax.ShapeDtypeStruct(value.shape, value.dtype) for value in values],
        input_output_aliases={at: at for at in range(len(values))},
        compiler_params=pltpu.CompilerParams(vmem_limit_bytes=1 << 20),
    )(*values, *gates)


def after(value, *others):
    return lax.optimization_barrier((value,) + others)[0]


def project(rows, adapter, mask):
    tenants, ranks, width = adapter.shape
    flat = adapter.reshape(tenants * ranks, width)
    parts = []
    for at, size in pieces(rows.shape[0]):
        full = dot(rows[at : at + size], flat, CONTRACT_LAST)
        chosen = full.reshape(size, tenants, ranks) * mask[at : at + size, :, None]
        parts.append(jnp.sum(chosen, axis=1))
    return jnp.concatenate(parts, axis=0).astype(jnp.bfloat16)


def spread(rank, mask):
    wide = rank[:, None, :] * mask.astype(jnp.bfloat16)[:, :, None]
    return wide.reshape(rank.shape[0], -1)


def adapter_grad(rank, mask, rows, weights):
    tenants, ranks = mask.shape[1], rank.shape[1]
    parts = []
    for at, size in pieces(tenants * ranks):
        low, high = at // ranks, (at + size) // ranks
        grad = dot(spread(rank, mask[:, low:high]), rows, CONTRACT_ROWS)
        parts.append(grad.reshape(high - low, ranks, -1) * weights[low:high, None, None])
    return jnp.concatenate(parts, axis=0)


def shards(grad_output, hidden, down_weight, adapter_down, adapter_up, job_tenant, job_count):
    index = lax.axis_index("seq")
    group = lax.axis_index("grp")
    count = lax.axis_size("seq")
    groups = lax.axis_size("grp")
    chips = count // CORES
    chip, core = index // CORES, index % CORES
    block = grad_output.shape[0]
    tenants, ranks, down_slab = adapter_down.shape
    up_slab = adapter_up.shape[2]
    width = down_weight.shape[0]
    part = block // groups

    named = (job_tenant[:, :, None] == jnp.arange(tenants, dtype=jnp.int32)).astype(jnp.float32)
    totals = jnp.sum(job_count.astype(jnp.float32)[:, :, None] * named, axis=(0, 1))
    weights = ADAPTER_SCALE / totals
    ends = jnp.cumsum(job_count, axis=1)
    places = jnp.arange(block, dtype=jnp.int32)[None, :, None]
    member = (places >= (ends - job_count)[:, None, :]) & (places < ends[:, None, :])
    owner = jnp.sum(jnp.where(member, job_tenant[:, None, :], 0), axis=2).reshape(count * block)
    mask = (owner[:, None] == jnp.arange(tenants, dtype=jnp.int32)).astype(jnp.float32)

    def seq_move(value, chips_back, flip):
        pairs = [
            (s, ((s // CORES - chips_back) % chips) * CORES + ((s % CORES) ^ flip))
            for s in range(count)
        ]
        return lax.ppermute(value, "seq", pairs)

    def grp_move(value, flip):
        return lax.ppermute(value, "grp", [(g, g ^ flip) for g in range(groups)])

    held = [grad_output]
    for step in range(1, chips):
        held.append(seq_move(held[-1], -1, 0))
    pairs = [(near, seq_move(near, 0, 1)) for near in held]

    hidden_slab = lax.all_to_all(
        hidden.reshape(block, count, down_slab).transpose(1, 0, 2),
        "seq",
        split_axis=0,
        concat_axis=0,
        tiled=True,
    ).reshape(count * block, down_slab)

    last = chips - 1
    products = [chunk_product(near, far, down_weight, group) for near, far in pairs]
    firsts = [
        (grp_move(near_sent, 1), grp_move(far_sent, 2)) for _, near_sent, _, far_sent in products
    ]
    grad_slab = jnp.zeros((count, block, up_slab), jnp.bfloat16)
    for step, pair in enumerate(pairs):
        back = ((chip - step) % chips) * CORES
        for flip, rows in enumerate(pair):
            columns = lax.dynamic_slice_in_dim(rows, index * up_slab, up_slab, 1)
            grad_slab = lax.dynamic_update_index_in_dim(grad_slab, columns, back + (core ^ flip), 0)
    grad_slab = grad_slab.reshape(count * block, up_slab)

    def second(step, *gates):
        near_kept, _, far_kept, _ = products[step]
        near_came, far_came = firsts[step]
        near_came, far_came = lax.optimization_barrier((near_came, far_came) + gates)[:2]
        near_sum = add(near_kept[1], near_came[1])
        far_sum = add(far_kept[1], far_came[1])
        return near_sum, (grp_move(near_sum, 2), grp_move(far_sum, 1))

    def total(step, seconds, *gates):
        near_kept, _, far_kept, _ = products[step]
        near_came, far_came = firsts[step]
        if step == last - 1:
            near_last, far_last = touch(seconds, *gates)
        else:
            near_last, far_last = lax.optimization_barrier(seconds + gates)[:2]
        return (
            add(near_kept[0], near_came[0], near_last),
            add(far_kept[0], far_came[0], far_last),
        )

    arrived = jnp.zeros((count, part, width), jnp.bfloat16)

    def hop(step, sums):
        return [
            sums[flip] if step == 0 and flip == 0 else seq_move(sums[flip], step, flip)
            for flip in range(CORES)
        ]

    def put(arrived, step, came, *gates):
        ahead = ((chip + step) % chips) * CORES
        came = lax.optimization_barrier(tuple(came) + gates)
        for flip in range(CORES):
            arrived = lax.dynamic_update_index_in_dim(arrived, came[flip], ahead + (core ^ flip), 0)
        return arrived

    came = None
    for step in range(last - 1):
        _, seconds = second(step, products[step + 1][0])
        sums = total(step, seconds)
        if came is not None:
            arrived = put(arrived, step - 1, came, sums[0])
        came = hop(step, sums)

    begun, seconds = second(last - 1, products[last][0])
    rows_here = lax.optimization_barrier((grad_slab, hidden_slab, begun))
    ranked = jnp.concatenate(
        [project(rows_here[0], adapter_up, mask), project(rows_here[1], adapter_down, mask)],
        axis=1,
    )
    devices = count * groups
    share = lax.all_to_all(
        ranked.reshape(devices, -1, 2 * ranks),
        ("grp", "seq"),
        split_axis=0,
        concat_axis=0,
        tiled=True,
    )
    sums = total(last - 1, seconds, share)
    arrived = put(arrived, last - 2, came, sums[0])
    came = hop(last - 1, sums)
    begun, seconds = second(last, sums[0])
    share = after(share, begun)
    share = jnp.sum(share.astype(jnp.float32), axis=0).astype(jnp.bfloat16)
    ranked = lax.all_to_all(
        jnp.broadcast_to(share[None], (devices,) + share.shape),
        ("grp", "seq"),
        split_axis=0,
        concat_axis=0,
        tiled=True,
    ).reshape(count * block, 2 * ranks)
    sums = total(last, seconds, share)
    arrived = put(arrived, last - 1, came, sums[0])
    came = hop(last, sums)
    ranked = after(ranked, *sums)
    grad_rank = ranked[:, :ranks]

    flat_down = adapter_down.reshape(tenants * ranks, down_slab)
    term = jnp.concatenate(
        [
            jnp.dot(
                spread(grad_rank[at : at + size], mask[at : at + size]),
                flat_down,
                preferred_element_type=jnp.float32,
            )
            for at, size in pieces(count * block)
        ],
        axis=0,
    )
    term = (term * ADAPTER_SCALE).astype(jnp.bfloat16).reshape(count, block, down_slab)
    arrived = put(arrived, last, came, term)
    rank_here = after(ranked, term)
    term = lax.all_to_all(term, "seq", split_axis=0, concat_axis=0, tiled=True)

    each = count // groups
    bases = []
    for flip in range(groups):
        sums = lax.dynamic_slice_in_dim(arrived, (group ^ flip) * each, each, 0)
        bases.append(grp_move(sums, flip) if flip else sums)

    grad_down = adapter_grad(rank_here[:, :ranks], mask, hidden_slab, weights)
    grad_up = adapter_grad(rank_here[:, ranks:], mask, grad_slab, weights)
    grad_hidden = join(bases, term, group)
    return grad_hidden, grad_down, grad_up


def solution(mesh):
    placed = (
        P("seq", "grp"),
        P("seq", "grp"),
        P("seq", "grp"),
        P(None, None, ("grp", "seq")),
        P(None, None, ("grp", "seq")),
        P(),
        P(),
    )
    return jax.shard_map(
        shards,
        mesh=mesh,
        in_specs=placed,
        out_specs=(P("seq", "grp"), P(None, None, ("grp", "seq")), P(None, None, ("grp", "seq"))),
        check_vma=False,
    )
```

```python
import functools

import jax
import jax.numpy as jnp
from jax import lax
from jax.experimental import pallas as pl
from jax.experimental.pallas import tpu as pltpu
from jax.sharding import PartitionSpec as P

ADAPTER_SCALE = 2.0
CONTRACT_LAST = (((1,), (1,)), ((), ()))
CONTRACT_ROWS = (((0,), (0,)), ((), ()))
CORES = 2
MOST_ROWS = 1024
ANYWHERE = pl.BlockSpec(memory_space=pl.ANY)


def dot(left, right, dims):
    return lax.dot_general(left, right, dims, preferred_element_type=jnp.float32)


def pieces(total):
    step = min(total, MOST_ROWS)
    return [(at, min(step, total - at)) for at in range(0, total, step)]


def tile_of(width):
    fits = [tile for tile in (512, 448, 384, 256, 128) if width % tile == 0 and tile % 128 == 0]
    return fits[0] if fits else width


def chunk_kernel(stages, place_ref, near_ref, far_ref, weight_ref, *rest):
    outs, rows = rest[:-1], rest[-1]
    part = near_ref.shape[0] // (2 * len(stages))
    sides = [(ref, flips) for ref, order in zip((near_ref, far_ref), stages) for flips in order]
    cuts = [(ref, flip) for ref, flips in sides for flip in flips]

    @pl.when(pl.program_id(0) == 0)
    def _():
        for at, (ref, flip) in enumerate(cuts):
            low = pl.multiple_of((place_ref[0] ^ flip) * part, part)
            rows[at * part : (at + 1) * part] = ref[pl.ds(low, part)]

    full = dot(rows[...], weight_ref[...], CONTRACT_LAST).astype(jnp.bfloat16)
    for at in range(len(cuts)):
        outs[at // 2][at % 2] = full[at * part : (at + 1) * part]


STAGES = (((0, 2), (1, 3)), ((0, 1), (2, 3)))


def chunk_product(near, far, weight, group):
    block, depth = near.shape
    width = weight.shape[0]
    tile = tile_of(width)
    part = block // (2 * len(STAGES))
    return pl.pallas_call(
        functools.partial(chunk_kernel, STAGES),
        grid_spec=pltpu.PrefetchScalarGridSpec(
            num_scalar_prefetch=1,
            grid=(width // tile,),
            in_specs=[
                pl.BlockSpec((block, depth), lambda at, place: (0, 0)),
                pl.BlockSpec((block, depth), lambda at, place: (0, 0)),
                pl.BlockSpec((tile, depth), lambda at, place: (at, 0)),
            ],
            out_specs=[pl.BlockSpec((2, part, tile), lambda at, place: (0, 0, at))] * 4,
            scratch_shapes=[pltpu.VMEM((CORES * block, depth), jnp.bfloat16)],
        ),
        out_shape=[jax.ShapeDtypeStruct((2, part, width), jnp.bfloat16)] * 4,
        compiler_params=pltpu.CompilerParams(vmem_limit_bytes=24 << 20),
        cost_estimate=pl.CostEstimate(
            flops=2 * CORES * block * depth * width,
            bytes_accessed=2 * (width * depth + CORES * block * (depth + width)),
            transcendentals=0,
        ),
    )(group.reshape(1), near, far, weight)


def join_kernel(groups, slab, place_ref, *refs):
    bases, term_ref, out_ref = refs[:groups], refs[groups], refs[groups + 1]
    width = bases[0].shape[2]
    for flip in range(groups):

        @pl.when(pl.program_id(0) == flip)
        def _():
            for at in range(term_ref.shape[0]):
                low = at * slab
                base = bases[flip][low // width, :, low % width : low % width + slab]
                total = base.astype(jnp.float32) + term_ref[at].astype(jnp.float32)
                out_ref[:, low : low + slab] = total.astype(jnp.bfloat16)


def join(bases, term, group):
    groups = len(bases)
    each, part, width = bases[0].shape
    count, block, slab = term.shape
    if slab % 128:
        base = jnp.zeros((groups, part, each, width), jnp.bfloat16)
        for flip, rows in enumerate(bases):
            base = lax.dynamic_update_index_in_dim(base, rows.transpose(1, 0, 2), group ^ flip, 0)
        total = base.reshape(block, -1).astype(jnp.float32)
        return (total + term.transpose(1, 0, 2).reshape(block, -1)).astype(jnp.bfloat16)
    return pl.pallas_call(
        functools.partial(join_kernel, groups, slab),
        grid_spec=pltpu.PrefetchScalarGridSpec(
            num_scalar_prefetch=1,
            grid=(groups,),
            in_specs=[pl.BlockSpec((each, part, width), lambda at, place: (0, 0, 0))] * groups
            + [pl.BlockSpec((count, part, slab), lambda at, place: (0, place[0] ^ at, 0))],
            out_specs=pl.BlockSpec((part, each * width), lambda at, place: (place[0] ^ at, 0)),
        ),
        out_shape=jax.ShapeDtypeStruct((block, each * width), jnp.bfloat16),
        compiler_params=pltpu.CompilerParams(vmem_limit_bytes=24 << 20),
        cost_estimate=pl.CostEstimate(
            flops=block * each * width, bytes_accessed=6 * block * each * width, transcendentals=0
        ),
    )(group.reshape(1), *bases, term)


def add(*terms):
    return sum(term.astype(jnp.float32) for term in terms).astype(jnp.bfloat16)


def touch_kernel(*refs):
    pass


def touch(values, *gates):
    return pl.pallas_call(
        touch_kernel,
        in_specs=[ANYWHERE] * (len(values) + len(gates)),
        out_specs=[ANYWHERE] * len(values),
        out_shape=[jax.ShapeDtypeStruct(value.shape, value.dtype) for value in values],
        input_output_aliases={at: at for at in range(len(values))},
        compiler_params=pltpu.CompilerParams(vmem_limit_bytes=1 << 20),
    )(*values, *gates)


def after(value, *others):
    return lax.optimization_barrier((value,) + others)[0]


def project(rows, adapter, mask):
    tenants, ranks, width = adapter.shape
    flat = adapter.reshape(tenants * ranks, width)
    parts = []
    for at, size in pieces(rows.shape[0]):
        full = dot(rows[at : at + size], flat, CONTRACT_LAST)
        chosen = full.reshape(size, tenants, ranks) * mask[at : at + size, :, None]
        parts.append(jnp.sum(chosen, axis=1))
    return jnp.concatenate(parts, axis=0).astype(jnp.bfloat16)


def spread(rank, mask):
    wide = rank[:, None, :] * mask.astype(jnp.bfloat16)[:, :, None]
    return wide.reshape(rank.shape[0], -1)


def adapter_grad(rank, mask, rows, weights):
    tenants, ranks = mask.shape[1], rank.shape[1]
    parts = []
    for at, size in pieces(tenants * ranks):
        low, high = at // ranks, (at + size) // ranks
        grad = dot(spread(rank, mask[:, low:high]), rows, CONTRACT_ROWS)
        parts.append(grad.reshape(high - low, ranks, -1) * weights[low:high, None, None])
    return jnp.concatenate(parts, axis=0)


def shards(grad_output, hidden, down_weight, adapter_down, adapter_up, job_tenant, job_count):
    index = lax.axis_index("seq")
    group = lax.axis_index("grp")
    count = lax.axis_size("seq")
    groups = lax.axis_size("grp")
    chips = count // CORES
    chip, core = index // CORES, index % CORES
    block = grad_output.shape[0]
    tenants, ranks, down_slab = adapter_down.shape
    up_slab = adapter_up.shape[2]
    width = down_weight.shape[0]
    part = block // groups

    named = (job_tenant[:, :, None] == jnp.arange(tenants, dtype=jnp.int32)).astype(jnp.float32)
    totals = jnp.sum(job_count.astype(jnp.float32)[:, :, None] * named, axis=(0, 1))
    weights = ADAPTER_SCALE / totals
    ends = jnp.cumsum(job_count, axis=1)
    places = jnp.arange(block, dtype=jnp.int32)[None, :, None]
    member = (places >= (ends - job_count)[:, None, :]) & (places < ends[:, None, :])
    owner = jnp.sum(jnp.where(member, job_tenant[:, None, :], 0), axis=2).reshape(count * block)
    mask = (owner[:, None] == jnp.arange(tenants, dtype=jnp.int32)).astype(jnp.float32)

    def seq_move(value, chips_back, flip):
        pairs = [
            (s, ((s // CORES - chips_back) % chips) * CORES + ((s % CORES) ^ flip))
            for s in range(count)
        ]
        return lax.ppermute(value, "seq", pairs)

    def grp_move(value, flip):
        return lax.ppermute(value, "grp", [(g, g ^ flip) for g in range(groups)])

    held = [grad_output]
    for step in range(1, chips):
        held.append(seq_move(held[-1], -1, 0))
    pairs = [(near, seq_move(near, 0, 1)) for near in held]

    hidden_slab = lax.all_to_all(
        hidden.reshape(block, count, down_slab).transpose(1, 0, 2),
        "seq",
        split_axis=0,
        concat_axis=0,
        tiled=True,
    ).reshape(count * block, down_slab)

    last = chips - 1
    products = [chunk_product(near, far, down_weight, group) for near, far in pairs]
    firsts = [
        (grp_move(near_sent, 1), grp_move(far_sent, 2)) for _, near_sent, _, far_sent in products
    ]
    grad_slab = jnp.zeros((count, block, up_slab), jnp.bfloat16)
    for step, pair in enumerate(pairs):
        back = ((chip - step) % chips) * CORES
        for flip, rows in enumerate(pair):
            columns = lax.dynamic_slice_in_dim(rows, index * up_slab, up_slab, 1)
            grad_slab = lax.dynamic_update_index_in_dim(grad_slab, columns, back + (core ^ flip), 0)
    grad_slab = grad_slab.reshape(count * block, up_slab)

    def second(step, *gates):
        near_kept, _, far_kept, _ = products[step]
        near_came, far_came = firsts[step]
        near_came, far_came = lax.optimization_barrier((near_came, far_came) + gates)[:2]
        near_sum = add(near_kept[1], near_came[1])
        far_sum = add(far_kept[1], far_came[1])
        return near_sum, (grp_move(near_sum, 2), grp_move(far_sum, 1))

    def total(step, seconds, *gates):
        near_kept, _, far_kept, _ = products[step]
        near_came, far_came = firsts[step]
        if step >= last - 1:
            near_last, far_last = touch(seconds, *gates)
        else:
            near_last, far_last = lax.optimization_barrier(seconds + gates)[:2]
        return (
            add(near_kept[0], near_came[0], near_last),
            add(far_kept[0], far_came[0], far_last),
        )

    arrived = jnp.zeros((count, part, width), jnp.bfloat16)

    def hop(step, sums):
        return [
            sums[flip] if step == 0 and flip == 0 else seq_move(sums[flip], step, flip)
            for flip in range(CORES)
        ]

    def put(arrived, step, came, *gates):
        ahead = ((chip + step) % chips) * CORES
        came = lax.optimization_barrier(tuple(came) + gates)
        for flip in range(CORES):
            arrived = lax.dynamic_update_index_in_dim(arrived, came[flip], ahead + (core ^ flip), 0)
        return arrived

    came = None
    for step in range(last - 1):
        _, seconds = second(step, products[step + 1][0])
        sums = total(step, seconds)
        if came is not None:
            arrived = put(arrived, step - 1, came, sums[0])
        came = hop(step, sums)

    begun, seconds = second(last - 1, products[last][0])
    rows_here = lax.optimization_barrier((grad_slab, hidden_slab, begun))
    ranked = jnp.concatenate(
        [project(rows_here[0], adapter_up, mask), project(rows_here[1], adapter_down, mask)],
        axis=1,
    )
    devices = count * groups
    share = lax.all_to_all(
        ranked.reshape(devices, -1, 2 * ranks),
        ("grp", "seq"),
        split_axis=0,
        concat_axis=0,
        tiled=True,
    )
    sums = total(last - 1, seconds, share)
    arrived = put(arrived, last - 2, came, sums[0])
    came = hop(last - 1, sums)
    begun, seconds = second(last, sums[0])
    share = after(share, begun)
    share = jnp.sum(share.astype(jnp.float32), axis=0).astype(jnp.bfloat16)
    ranked = lax.all_to_all(
        jnp.broadcast_to(share[None], (devices,) + share.shape),
        ("grp", "seq"),
        split_axis=0,
        concat_axis=0,
        tiled=True,
    ).reshape(count * block, 2 * ranks)
    sums = total(last, seconds, ranked)
    before, came = came, hop(last, sums)
    ranked = after(ranked, *sums)
    grad_rank = ranked[:, :ranks]

    flat_down = adapter_down.reshape(tenants * ranks, down_slab)
    term = jnp.concatenate(
        [
            jnp.dot(
                spread(grad_rank[at : at + size], mask[at : at + size]),
                flat_down,
                preferred_element_type=jnp.float32,
            )
            for at, size in pieces(count * block)
        ],
        axis=0,
    )
    term = (term * ADAPTER_SCALE).astype(jnp.bfloat16).reshape(count, block, down_slab)
    arrived = put(arrived, last - 1, touch(before, term))
    arrived = put(arrived, last, touch(came, term))
    rank_here = after(ranked, term)
    term = lax.all_to_all(term, "seq", split_axis=0, concat_axis=0, tiled=True)

    each = count // groups
    bases = []
    for flip in range(groups):
        sums = lax.dynamic_slice_in_dim(arrived, (group ^ flip) * each, each, 0)
        bases.append(grp_move(sums, flip) if flip else sums)

    grad_down = adapter_grad(rank_here[:, :ranks], mask, hidden_slab, weights)
    grad_up = adapter_grad(rank_here[:, ranks:], mask, grad_slab, weights)
    grad_hidden = join(bases, term, group)
    return grad_hidden, grad_down, grad_up


def solution(mesh):
    placed = (
        P("seq", "grp"),
        P("seq", "grp"),
        P("seq", "grp"),
        P(None, None, ("grp", "seq")),
        P(None, None, ("grp", "seq")),
        P(),
        P(),
    )
    return jax.shard_map(
        shards,
        mesh=mesh,
        in_specs=placed,
        out_specs=(P("seq", "grp"), P(None, None, ("grp", "seq")), P(None, None, ("grp", "seq"))),
        check_vma=False,
    )
```
